128 devices in a mesh: replica: 16 (over z_lo, x, core), fsdp: 8 (over y, z_hi).
Axes of the slice: x: 4, y: 4, z: 4 (z_hi: 2, z_lo: 2; z = z_hi * 2 + z_lo), core: 2. Of those that a mesh axis runs over, the one named last changes fastest.
Arguments:
- context: bfloat16 [65536, 2048], P(('replica', 'fsdp')), may hold values from -6 to 6
- cotangent: bfloat16 [65536, 3584], P(('replica', 'fsdp')), may hold values from -60 to 60
- weight: bfloat16 [16, 2048, 3584], P('replica', 'fsdp'), may hold values from -0.125 to 0.125
- gain: float32 [16, 3584], P('replica'), may hold values from 0.1 to 1.9
- delta: float32 [16, 2048, 3584], P('replica', 'fsdp'), may hold values from -6 to 6
- anchor: float32 [2048, 3584], P('fsdp', 'replica'), may hold values from -6 to 6
- momentum: float32 [2048, 3584], P('fsdp', 'replica'), may hold values from -6 to 6
Outputs:
- grad_context: bfloat16 [65536, 2048], P(('replica', 'fsdp'))
- grad_weight: float32 [16, 2048, 3584], P('replica', 'fsdp')
- grad_gain: float32 [16, 3584], P('replica')
- new_anchor: float32 [2048, 3584], P('fsdp', 'replica')
- new_momentum: float32 [2048, 3584], P('fsdp', 'replica')
The draws below stay inside these ranges and needn't reach their ends.
All inputs are finite; a program needn't handle non-finite values.
Results may differ from the reference program's by a relative error of at most 0.014.
Values may be sent and summed in bfloat16 or wider, within the bound.
No kernel may reach another device: no remote copies, remote signals or barrier semaphores. Data moves between devices by JAX's collectives and lax.ppermute only.
A program may use at most 128 MiB of HBM per device.

```python
import jax
import jax.numpy as jnp
from jax import lax

D = 3584
HD = 2048
TOK_DEV = 512
TOKENS = 4096
ROWS = 65536
FRAG = 2048
N_REPLICA = 16
N_FSDP = 8


def draw_cotangent(key, part):
    key = jax.random.fold_in(key, 11)
    first, second, third = jax.random.split(key, 3)
    base = jax.random.truncated_normal(first, -4.0, 4.0, (ROWS, D), jnp.float32)
    row_scale = jnp.exp(jax.random.uniform(second, (ROWS, 1), jnp.float32) * jnp.log(10.0))
    column_scale = jnp.exp(jax.random.uniform(third, (1, D), jnp.float32) * jnp.log(10.0))
    position = (jnp.arange(ROWS) % TOKENS).astype(jnp.float32) / (TOKENS - 1)
    rising = jnp.exp(position * jnp.log(3.0))[:, None]
    return (0.05 * base * row_scale * column_scale * rising).astype(jnp.bfloat16)


def with_spikes(result, stream_key, source, target, blocks, factor):
    owner, partner = [(jnp.arange(result.shape[dim]) // (result.shape[dim] // blocks)).reshape([-1 if axis == dim else 1 for axis in range(result.ndim)]) for dim in (source, target)]
    chosen = jax.random.permutation(stream_key, blocks)[partner]
    strong = (owner == chosen) | (owner == (partner + blocks // 2) % blocks)
    return jnp.where(strong, factor * result, result)


def block_scale(key, dims, cuts, low, high):
    level = 1.0
    for axis_at, parts in cuts:
        steps = jax.random.uniform(jax.random.fold_in(jax.random.fold_in(key, 6), axis_at), (parts,), jnp.float32, low / len(cuts), high / len(cuts))
        level = level * jnp.repeat(jnp.exp(steps), dims[axis_at] // parts).reshape((-1,) + (1,) * (len(dims) - 1 - axis_at))
    return level


def noise(stream_key, dims, width, most, shards=(), held_as=jnp.bfloat16):
    drawn = width * jax.random.normal(stream_key, dims, jnp.float32)
    if shards:
        drawn = drawn * block_scale(stream_key, dims, shards, -0.22, 0.18)
    return jnp.clip(drawn, -most, most).astype(held_as)


def gaussian_with(rng, extent, width, most, cuts, heavy, dtype=jnp.bfloat16):
    drawn = width * jax.random.normal(rng, extent, jnp.float32)
    if cuts:
        drawn = drawn * block_scale(rng, extent, cuts, -0.22, 0.18)
    return jnp.clip(with_spikes(drawn, jax.random.fold_in(rng, 3), *heavy), -most, most).astype(dtype)


def setup_inputs(seed: int = 0) -> dict:
    seeds = jax.random.split(jax.random.key(seed), 8)
    return {
        "context": noise(seeds[0], (ROWS, HD), 1.0, 6.0, ((0, 128),)),
        "cotangent": draw_cotangent(jax.random.fold_in(seeds[7], 71), 0),
        "weight": noise(seeds[2], (N_REPLICA, HD, D), HD ** -0.5, 0.125, ((0, 16), (1, 8))),
        "gain": jnp.clip(1.0 + 0.18 * jax.random.normal(seeds[3], (N_REPLICA, D), jnp.float32), 0.1, 1.9),
        "delta": gaussian_with(seeds[4], (N_REPLICA, FRAG, D), 1.0, 6.0, ((0, 16), (1, 8)), (0, 2, 16, 2.0), jnp.float32),
        "anchor": noise(seeds[5], (FRAG, D), 1.0, 6.0, ((0, 8), (1, 16)), jnp.float32),
        "momentum": noise(seeds[6], (FRAG, D), 0.5, 6.0, ((0, 8), (1, 16)), jnp.float32),
    }


def replica_step(inputs):
    context, cotangent, weight, gain = inputs
    projected = jnp.dot(context, weight, preferred_element_type=jnp.float32)
    inverse = lax.rsqrt(lax.optimization_barrier(jnp.mean(projected * projected, axis=-1, keepdims=True)) + 1e-06)
    normed = projected * inverse
    cot_float = cotangent.astype(jnp.float32)
    scaled = cot_float * gain
    grad_out = ((scaled - normed * lax.optimization_barrier(jnp.mean(scaled * normed, axis=-1, keepdims=True))) * inverse).astype(jnp.bfloat16)
    grad_context = lax.dot_general(grad_out, weight, (((1,), (1,)), ((), ())), preferred_element_type=jnp.float32).astype(jnp.bfloat16)
    grad_gain = lax.optimization_barrier(jnp.sum(cot_float * normed, axis=0))
    context_blocks = context.reshape(N_FSDP, TOK_DEV, HD)
    grad_blocks = grad_out.reshape(N_FSDP, TOK_DEV, D)

    def add_block(running, blocks):
        term = lax.dot_general(blocks[0], blocks[1], (((0,), (0,)), ((), ())), preferred_element_type=jnp.float32)
        rounded = lax.optimization_barrier(term.astype(jnp.bfloat16))
        return (running + rounded.astype(jnp.float32), None)
    grad_weight, _ = lax.scan(add_block, jnp.zeros((HD, D), jnp.float32), (context_blocks, grad_blocks))
    return (grad_context, grad_weight, grad_gain)

def reference(context, cotangent, weight, gain, delta, anchor, momentum):
    grad_context, grad_weight, grad_gain = lax.map(replica_step, (context.reshape(N_REPLICA, TOKENS, HD), cotangent.reshape(N_REPLICA, TOKENS, D), weight, gain))
    outer_grad = lax.optimization_barrier(jnp.sum(delta, axis=0)) / N_REPLICA
    new_momentum = 0.9 * momentum + outer_grad
    new_anchor = anchor - 0.7 * (outer_grad + 0.9 * new_momentum)
    return (grad_context.reshape(ROWS, HD), grad_weight, grad_gain, new_anchor, new_momentum)
```

```python
import jax
import jax.numpy as jnp
from jax import lax
from jax.sharding import PartitionSpec as P

BF16 = jnp.bfloat16
F32 = jnp.float32
BOTH = ("replica", "fsdp")


def partner_y(y, core):
    if core == 0:
        return y ^ 1
    return (y - 1) % 4 if y % 2 == 0 else (y + 1) % 4


def table(move):
    pairs = []
    for r in range(16):
        for f in range(8):
            z_lo, x, core, y, z_hi = r // 8, (r // 2) % 4, r % 2, f // 2, f % 2
            z_lo, x, core, y, z_hi = move(z_lo, x, core, y, z_hi)
            pairs.append((r * 8 + f, ((z_lo * 4 + x) * 2 + core) * 8 + y * 2 + z_hi))
    return pairs


TO_PARTNER = table(lambda a, x, c, y, z: (a, x, c, partner_y(y, c), z))
TO_MATE = table(lambda a, x, c, y, z: (a, x, c, partner_y(y, 1 - c), z))
TO_Z = table(lambda a, x, c, y, z: (a, x, c, y, 1 - z))
TO_CORE = table(lambda a, x, c, y, z: (a, x, 1 - c, y, z))
TO_X1 = table(lambda a, x, c, y, z: (a, x ^ 1, c, y, z))
TO_X3 = table(lambda a, x, c, y, z: (a, 3 - x, c, y, z))
TO_ZLO = table(lambda a, x, c, y, z: (1 - a, x, c, y, z))


def send(value, pairs):
    return lax.ppermute(value, BOTH, pairs)


def pick(stack, index):
    return lax.dynamic_index_in_dim(stack, index, 0, keepdims=False)


def outer_update(delta, anchor, momentum):
    r = lax.axis_index("replica")
    z_lo, x, core = r // 8, (r // 2) % 4, r % 2
    parts = jnp.transpose(delta[0].reshape(256, 8, 2, 224), (2, 1, 0, 3))
    got = send(pick(parts, 1 - core).astype(BF16), TO_CORE)
    sums = (pick(parts, core) + got.astype(F32)).reshape(2, 4, 256, 224)
    by_x = jnp.transpose(sums, (1, 0, 2, 3))
    away = jnp.stack([pick(by_x, x ^ 1), pick(by_x, 3 - (x ^ 1))])
    got = send(away.astype(BF16), TO_X1)
    kept = jnp.stack([pick(by_x, x), pick(by_x, 3 - x)]) + got.astype(F32)
    got = send(kept[1].astype(BF16), TO_X3)
    kept = kept[0] + got.astype(F32)
    got = send(pick(kept, 1 - z_lo).astype(BF16), TO_ZLO)
    total = pick(kept, z_lo) + got.astype(F32)
    outer_grad = total / 16
    new_momentum = 0.9 * momentum + outer_grad
    new_anchor = anchor - 0.7 * (outer_grad + 0.9 * new_momentum)
    return (new_anchor, new_momentum)


def inner_step(context, cotangent, weight, gain):
    core = lax.axis_index("replica") % 2
    f = lax.axis_index("fsdp")
    y, z = f // 2, f % 2
    even = y % 2 == 0
    low, high = y ^ 1, jnp.where(even, (y + 3) % 4, (y + 1) % 4)
    partner = jnp.where(core == 0, low, high)
    mate = jnp.where(core == 0, high, low)
    opposite = (y + 2) % 4
    half = jnp.where(core == 0, ((y + 1) // 2) % 2, y // 2)

    def columns(array, which):
        return lax.dynamic_slice_in_dim(array, which * 1792, 1792, array.ndim - 1)

    own = columns(weight[0], half)
    other = columns(weight[0], 1 - half)

    from_partner = send(other, TO_PARTNER)
    from_mate = send(own, TO_MATE)
    own_z = send(own, TO_Z)
    context_p = send(context, TO_PARTNER)
    from_opposite = send(from_partner, TO_MATE)
    mate_z = send(from_mate, TO_Z)
    partner_z = send(from_partner, TO_Z)
    opposite_z = send(from_opposite, TO_Z)
    cot_p = send(columns(cotangent, 1 - half), TO_PARTNER)

    tokens = jnp.concatenate([context, context_p], axis=0)
    cot = jnp.concatenate([columns(cotangent, half), cot_p], axis=0).astype(F32)

    def slab(owner, zz):
        return lax.dynamic_slice_in_dim(tokens, (owner * 2 + zz) * 256, 256, 1)

    blocks = [
        (own, y, z),
        (from_mate, mate, z),
        (from_partner, partner, z),
        (from_opposite, opposite, z),
        (own_z, y, 1 - z),
        (mate_z, mate, 1 - z),
        (partner_z, partner, 1 - z),
        (opposite_z, opposite, 1 - z),
    ]
    projected = None
    for block, owner, zz in blocks:
        term = jnp.dot(slab(owner, zz), block, preferred_element_type=F32)
        projected = term if projected is None else projected + term

    scaled = cot * columns(gain[0], half)
    stats = jnp.stack(
        [jnp.sum(projected * projected, axis=-1), jnp.sum(scaled * projected, axis=-1)]
    )
    stats_p = send(stats, TO_PARTNER)
    stats = stats + jnp.concatenate([stats_p[:, 512:], stats_p[:, :512]], axis=1)
    inverse = lax.rsqrt(stats[0] / 3584 + 1e-06)
    coupling = stats[1] / 3584 * inverse
    normed = projected * inverse[:, None]
    grad_out = ((scaled - normed * coupling[:, None]) * inverse[:, None]).astype(BF16)

    def weight_term(owner, zz):
        return lax.dot_general(
            slab(owner, zz), grad_out, (((0,), (0,)), ((), ())), preferred_element_type=F32
        )

    o_mate = send(weight_term(mate, z).astype(BF16), TO_MATE)
    x_mate_z = send(weight_term(opposite, 1 - z).astype(BF16), TO_Z)
    o_mate_z = send(weight_term(mate, 1 - z).astype(BF16), TO_MATE)
    x_self_z = send(weight_term(partner, 1 - z).astype(BF16), TO_Z)

    def context_term(rows):
        parts = []
        for block, owner, zz in blocks:
            parts.append(
                lax.dot_general(
                    rows, block, (((1,), (1,)), ((), ())), preferred_element_type=F32
                )
            )
        return parts

    part_p = context_term(grad_out[512:])
    place = [owner * 2 + zz for _, owner, zz in blocks]

    def arrange(parts, dtype):
        whole = jnp.zeros((512, 2048), dtype)
        for part, at in zip(parts, place):
            whole = lax.dynamic_update_slice_in_dim(whole, part.astype(dtype), at * 256, 1)
        return whole

    got_context = send(arrange(part_p, BF16), TO_PARTNER)

    x_mate = (weight_term(opposite, z) + x_mate_z.astype(F32)).astype(BF16)
    x_from_mate = send(x_mate, TO_MATE)
    o_self_z = (weight_term(y, 1 - z) + o_mate_z.astype(F32)).astype(BF16)
    o_from_z = send(o_self_z, TO_Z)
    x_self = weight_term(partner, z) + x_self_z.astype(F32) + x_from_mate.astype(F32)
    x_got = send(x_self.astype(BF16), TO_PARTNER)
    o_self = weight_term(y, z) + o_mate.astype(F32) + o_from_z.astype(F32)
    x_got = x_got.astype(F32)

    grad_weight = jnp.concatenate(
        [jnp.where(half == 0, o_self, x_got), jnp.where(half == 0, x_got, o_self)], axis=1
    )

    grad_context = (
        arrange(context_term(grad_out[:512]), F32) + got_context.astype(F32)
    ).astype(BF16)

    gain_part = jnp.sum(cot * normed, axis=0)
    gain_part = gain_part + send(gain_part, TO_Z)
    gain_part = gain_part + send(gain_part, TO_MATE)
    gain_other = send(gain_part, TO_PARTNER)
    grad_gain = jnp.concatenate(
        [jnp.where(half == 0, gain_part, gain_other), jnp.where(half == 0, gain_other, gain_part)]
    )
    return (grad_context, grad_weight[None], grad_gain[None])


def per_device(context, cotangent, weight, gain, delta, anchor, momentum):
    new_anchor, new_momentum = outer_update(delta, anchor, momentum)
    grad_context, grad_weight, grad_gain = inner_step(context, cotangent, weight, gain)
    return (grad_context, grad_weight, grad_gain, new_anchor, new_momentum)


def solution(mesh):
    placed = (
        P(("replica", "fsdp"), None),
        P(("replica", "fsdp"), None),
        P("replica", "fsdp", None),
        P("replica", None),
        P("replica", "fsdp", None),
        P("fsdp", "replica"),
        P("fsdp", "replica"),
    )
    return jax.shard_map(
        per_device,
        mesh=mesh,
        in_specs=placed,
        out_specs=(
            P(("replica", "fsdp"), None),
            P("replica", "fsdp", None),
            P("replica", None),
            P("fsdp", "replica"),
            P("fsdp", "replica"),
        ),
        check_vma=False,
    )
```

```python
import jax
import jax.numpy as jnp
from jax import lax
from jax.experimental import pallas as pl
from jax.experimental.pallas import tpu as pltpu
from jax.sharding import PartitionSpec as P

BF16 = jnp.bfloat16
F32 = jnp.float32
BOTH = ("replica", "fsdp")
HALF = 1792
COLS = 224
WIDE = 256
TILE = 256
TILES = HALF // TILE
LIMIT = 10 * 2**20


def partner_y(y, core):
    if core == 0:
        return y ^ 1
    return (y - 1) % 4 if y % 2 == 0 else (y + 1) % 4


def table(move):
    pairs = []
    for r in range(16):
        for f in range(8):
            z_lo, x, core, y, z_hi = r // 8, (r // 2) % 4, r % 2, f // 2, f % 2
            z_lo, x, core, y, z_hi = move(z_lo, x, core, y, z_hi)
            pairs.append((r * 8 + f, ((z_lo * 4 + x) * 2 + core) * 8 + y * 2 + z_hi))
    return pairs


TO_PARTNER = table(lambda a, x, c, y, z: (a, x, c, partner_y(y, c), z))
TO_MATE = table(lambda a, x, c, y, z: (a, x, c, partner_y(y, 1 - c), z))
TO_Z = table(lambda a, x, c, y, z: (a, x, c, y, 1 - z))
TO_CORE = table(lambda a, x, c, y, z: (a, x, 1 - c, y, z))
TO_X1 = table(lambda a, x, c, y, z: (a, x ^ 1, c, y, z))
TO_X3 = table(lambda a, x, c, y, z: (a, 3 - x, c, y, z))
TO_ZLO = table(lambda a, x, c, y, z: (1 - a, x, c, y, z))


def send(value, pairs):
    return lax.ppermute(value, BOTH, pairs)


def after(value, *others):
    return lax.optimization_barrier((value, *others))[0]


HELD = pl.BlockSpec(memory_space=pltpu.VMEM)


def near(x):
    return pltpu.with_memory_space_constraint(x, pltpu.VMEM)


def far(x):
    return pltpu.with_memory_space_constraint(x, pltpu.HBM)


def call(kernel, name, cost, out_shape, grid, in_specs, out_specs, scratch=(), aliases=None):
    built = pl.pallas_call(
        kernel,
        out_shape=out_shape,
        grid_spec=pltpu.PrefetchScalarGridSpec(
            num_scalar_prefetch=1,
            grid=grid,
            in_specs=in_specs,
            out_specs=out_specs,
            scratch_shapes=list(scratch),
        ),
        compiler_params=pltpu.CompilerParams(vmem_limit_bytes=LIMIT),
        cost_estimate=pl.CostEstimate(flops=0, bytes_accessed=int(cost * 3e6), transcendentals=0),
        input_output_aliases=aliases or {},
        name=name,
    )

    def run(at, *operands):
        placed = [near(x) if spec is HELD else far(x) for x, spec in zip(operands, in_specs)]
        return built(at, *placed)

    return run


def split_kernel(at_ref, in_ref, own_ref, other_ref, sems):
    copies = []
    rows = own_ref.shape[0] // 4
    for i in range(4):
        for s, (out_ref, half) in enumerate(((own_ref, at_ref[0]), (other_ref, 1 - at_ref[0]))):
            part = pl.ds(i * rows, rows)
            lanes = pl.ds(pl.multiple_of(half * HALF, 256), HALF)
            copies.append(
                pltpu.make_async_copy(in_ref.at[part, lanes], out_ref.at[part], sems.at[s, i])
            )
    for copy in copies:
        copy.start()
    for copy in copies:
        copy.wait()


def split(which, array):
    return call(
        split_kernel,
        "split", 2,
        [pltpu.VMEM((array.shape[0], HALF), BF16)] * 2,
        (1,),
        [pl.BlockSpec(memory_space=pl.ANY)],
        [HELD] * 2,
        [pltpu.SemaphoreType.DMA((2, 4))],
    )(which, array)


def turn_kernel(at_ref, own_ref, partner_ref, out_ref, slab_ref):
    for k in range(8):
        at = pl.ds(pl.multiple_of(at_ref[k] * 256, 256), 256)
        out_ref[k * 256 : (k + 1) * 256, :512] = jnp.transpose(own_ref[:, at])
        out_ref[k * 256 : (k + 1) * 256, 512:] = jnp.transpose(partner_ref[:, at])
    at = pl.ds(pl.multiple_of(at_ref[0] * 256, 256), 256)
    slab_ref[:512] = own_ref[:, at]
    slab_ref[512:] = partner_ref[:, at]


def turn(at, context, context_p):
    return call(
        turn_kernel,
        "turn", 4,
        [pltpu.VMEM((2048, 1024), BF16), pltpu.VMEM((1024, 256), BF16)],
        (1,),
        [HELD, HELD],
        [HELD, HELD],
    )(at, context, context_p)


def outer_parts_kernel(at_ref, delta_ref, low_ref, high_ref, kept_ref):
    rows = pl.ds(pl.multiple_of(pl.program_id(0) * 64, 64), 64)
    for core in range(2):

        @pl.when(at_ref[0] == core)
        def _(core=core):
            for k in range(8):
                away, kept = (2 * k + 1 - core) * COLS, (2 * k + core) * COLS
                away_ref = low_ref if k < 4 else high_ref
                away_ref[k % 4, rows, :COLS] = delta_ref[:, away : away + COLS].astype(BF16)
                kept_ref[k, rows, :COLS] = delta_ref[:, kept : kept + COLS]


def outer_parts(at, delta):
    return call(
        outer_parts_kernel,
        "outer_parts", 3,
        [pltpu.VMEM((4, 256, WIDE), BF16)] * 2 + [pltpu.VMEM((8, 256, WIDE), F32)],
        (4,),
        [pl.BlockSpec((64, 16 * COLS), lambda i, at: (i, 0))],
        [HELD, HELD, HELD],
    )(at, delta)


def outer_sum_kernel(at_ref, kept_in_ref, *refs, turned):
    *got_refs, away_ref, kept_ref = refs
    n = away_ref.shape[0]
    view = jnp.transpose if turned else lambda block: block

    def total(i, at):
        piece = i * len(got_refs) // n
        got = got_refs[piece][at - piece * got_refs[0].shape[0]]
        return view(kept_in_ref[at] + got.astype(F32))

    for i in range(n):
        away_ref[i] = total(i, at_ref[i]).astype(BF16)
        kept_ref[i] = total(i, at_ref[n + i])


def outer_sum(at, kept, *got, turned=False):
    n = at.shape[0] // 2

    def kernel(*refs):
        outer_sum_kernel(*refs, turned=turned)

    return call(
        kernel,
        "outer_sum", 1,
        [pltpu.VMEM((n, 256, WIDE), BF16), pltpu.VMEM((n, 256, WIDE), F32)],
        (1,),
        [HELD] * (1 + len(got)),
        [HELD, HELD],
    )(at, kept, *got)


def slabs(at_ref, block_refs):
    k = 0
    for ref in block_refs:
        for row in range(0, ref.shape[0], 256):
            yield ref, row, pl.ds(pl.multiple_of(at_ref[k] * 256, 256), 256)
            k += 1


def project_kernel(at_ref, own_ref, partner_ref, *refs):
    *block_refs, out_ref = refs
    for j in range(TILES):
        lanes = slice(j * TILE, (j + 1) * TILE)
        for s, rows_ref in enumerate((own_ref, partner_ref)):
            total = None
            for ref, row, at in slabs(at_ref, block_refs):
                term = jnp.dot(
                    rows_ref[:, at], ref[row : row + 256, lanes], preferred_element_type=F32
                )
                total = term if total is None else total + term
            out_ref[s * 512 : (s + 1) * 512, lanes] = total


def project(at, context, context_p, blocks):
    return call(
        project_kernel,
        "project", 14,
        pltpu.VMEM((1024, HALF), F32),
        (1,),
        [HELD] * (2 + len(blocks)),
        HELD,
    )(at, context, context_p, *blocks)


def gain_lanes(at_ref, j):
    return pl.ds(pl.multiple_of(at_ref[8] * HALF + j * TILE, TILE), TILE)


def stats_kernel(at_ref, acc_ref, slab_ref, block_ref, cot_ref, cot_p_ref, gain_ref, out_ref):
    for s in range(4):
        rows = slice(s * 256, (s + 1) * 256)
        part = slice((s % 2) * 256, (s % 2 + 1) * 256)
        c_ref = cot_ref if s < 2 else cot_p_ref
        squares = jnp.zeros((256, 128), F32)
        products = jnp.zeros((256, 128), F32)
        for j in range(TILES):
            lanes = slice(j * TILE, (j + 1) * TILE)
            p = acc_ref[rows, lanes] + jnp.dot(
                slab_ref[rows], block_ref[:, lanes], preferred_element_type=F32
            )
            scaled = c_ref[part, lanes].astype(F32) * gain_ref[:, gain_lanes(at_ref, j)] * p
            p = p * p
            squares += p[:, :128] + p[:, 128:]
            products += scaled[:, :128] + scaled[:, 128:]
        for i in range(2):
            chunk = slice(i * 128, (i + 1) * 128)
            top = jnp.sum(jnp.transpose(squares[chunk]), axis=0, keepdims=True)
            low = jnp.sum(jnp.transpose(products[chunk]), axis=0, keepdims=True)
            out_ref[2 * s + i] = jnp.concatenate([top] * 4 + [low] * 4, axis=0)


def row_stats(at, acc, slab, block, cot, cot_p, gain):
    return call(
        stats_kernel,
        "row_stats", 3,
        pltpu.VMEM((8, 8, 128), F32),
        (1,),
        [HELD] * 6,
        HELD,
    )(at, acc, slab, block, cot, cot_p, gain)


def two_parts(value):
    high = value.astype(BF16).astype(F32)
    row = lax.broadcasted_iota(jnp.int32, (16, value.shape[1]), 0)
    return jnp.where(row == 0, high, jnp.where(row == 1, value - high, 0.0)).astype(BF16)


def one_value(rows):
    return jnp.sum(rows.astype(F32), axis=0, keepdims=True)


def grad_kernel(
    at_ref, acc_ref, slab_ref, block_ref, cot_ref, cot_p_ref, gain_ref, mine_ref, theirs_ref,
    turned_ref,
    g_ref, x_mate_ref, o_z_ref, a_ref, b_ref,
):
    for i in range(8):
        total = mine_ref[i] + theirs_ref[(i + 4) % 8]
        inverse = lax.rsqrt(total[0:1] / 3584 + 1e-06)
        coupling = total[4:5] / 3584 * inverse * inverse * inverse
        rows = pl.ds(i * 128, 128)
        a_ref[rows, :] = jnp.transpose(jnp.broadcast_to(inverse, (128, 128)))
        b_ref[rows, :] = jnp.transpose(jnp.broadcast_to(coupling, (128, 128)))

    for j in range(TILES):
        lanes = slice(j * TILE, (j + 1) * TILE)
        block = block_ref[:, lanes]
        gain = gain_ref[:, gain_lanes(at_ref, j)]
        gain_total = jnp.zeros((8, TILE), F32)
        for i in range(4):
            rows = slice(i * 256, (i + 1) * 256)
            part = slice((i % 2) * 256, (i % 2 + 1) * 256)
            c_ref = cot_ref if i < 2 else cot_p_ref
            p = acc_ref[rows, lanes] + jnp.dot(slab_ref[rows], block, preferred_element_type=F32)
            inverse = jnp.concatenate([a_ref[rows]] * 2, axis=1)
            coupling = jnp.concatenate([b_ref[rows]] * 2, axis=1)
            cot = c_ref[part, lanes].astype(F32) * inverse
            g_ref[rows, lanes] = (cot * gain - p * coupling).astype(BF16)
            gain_total += jnp.sum((cot * p).reshape(32, 8, TILE), axis=0)
        terms = jnp.dot(turned_ref[:512], g_ref[:, lanes], preferred_element_type=F32)
        terms = terms.astype(BF16)
        x_mate_ref[:256, lanes] = terms[:256]
        x_mate_ref[256:, lanes] = two_parts(jnp.sum(gain_total, axis=0, keepdims=True))
        o_z_ref[:, lanes] = terms[256:]


def grad_step(at, acc, slab, block, cot, cot_p, gain, mine, theirs, turned):
    return call(
        grad_kernel,
        "grad_step", 6,
        (
            pltpu.VMEM((1024, HALF), BF16),
            pltpu.VMEM((272, HALF), BF16),
            pltpu.VMEM((256, HALF), BF16),
        ),
        (1,),
        [HELD] * 9,
        [HELD] * 3,
        [pltpu.VMEM((1024, 128), F32), pltpu.VMEM((1024, 128), F32)],
    )(at, acc, slab, block, cot, cot_p, gain, mine, theirs, turned)


def weight_kernel(at_ref, turned_ref, g_ref, *out_refs, first):
    n = len(out_refs)
    for j in range(TILES):
        lanes = slice(j * TILE, (j + 1) * TILE)
        terms = jnp.dot(
            turned_ref[first * 256 : (first + n) * 256],
            g_ref[:, lanes],
            preferred_element_type=F32,
        )
        for k, out_ref in enumerate(out_refs):
            out_ref[:, lanes] = terms[k * 256 : (k + 1) * 256].astype(out_ref.dtype)


def weight_terms(at, turned, g, first, n, dtype):
    def kernel(*refs):
        weight_kernel(*refs, first=first)

    return call(
        kernel,
        "weight_terms", n,
        [pltpu.VMEM((256, HALF), dtype)] * n,
        (1,),
        [HELD, HELD],
        [HELD] * n,
    )(at, turned, g)


def context_kernel(at_ref, g_ref, *refs, first):
    *block_refs, out_ref = refs
    rows = slice(first, first + out_ref.shape[0])
    for ref, row, at in slabs(at_ref, block_refs):
        part = lax.dot_general(
            g_ref[rows, :],
            ref[row : row + 256],
            (((1,), (1,)), ((), ())),
            preferred_element_type=F32,
        )
        out_ref[:, at] = part.astype(out_ref.dtype)


def context_term(at, g, first, blocks, dtype, tiles):
    def kernel(*refs):
        context_kernel(*refs, first=first)

    return call(
        kernel,
        "context_term", 2.5 * tiles,
        pltpu.VMEM((256 * tiles, 2048), dtype),
        (1,),
        [HELD] * (1 + len(blocks)),
        HELD,
    )(at, g, *blocks)


def add_kernel(at_ref, a_ref, b_ref, out_ref):
    out_ref[...] = (a_ref[...] + b_ref[...].astype(F32)).astype(BF16)


def add(at, a, b):
    return call(
        add_kernel, "add", 1, pltpu.VMEM((256, HALF), BF16), (1,), [HELD, HELD], HELD
    )(at, a, b)


def add_x_kernel(at_ref, a_ref, *refs):
    *in_refs, high_ref, low_ref = refs
    sent_ref, *got_refs = in_refs
    total = a_ref[...]
    if got_refs[0].shape[0] == 128:
        got = jnp.concatenate([got_refs[0][...], got_refs[1][:128]], axis=0)
        sums_ref, more = got_refs[1], got_refs[2:]
    else:
        got = got_refs[0][:256]
        sums_ref, more = got_refs[0], got_refs[1:]
    total = total + got.astype(F32)
    for ref in more:
        total = total + ref[...].astype(F32)
    high_ref[...] = total[:128].astype(BF16)
    low_ref[:128] = total[128:].astype(BF16)
    sums = one_value(sent_ref[sent_ref.shape[0] - 16 :])
    low_ref[128:] = two_parts(sums + one_value(sums_ref[sums_ref.shape[0] - 16 :]))


def add_x(at, own, sent, *got):
    return call(
        add_x_kernel,
        "add_x", 1,
        [pltpu.VMEM((128, HALF), BF16), pltpu.VMEM((144, HALF), BF16)],
        (1,),
        [HELD] * (2 + len(got)),
        [HELD, HELD],
    )(at, own, sent, *got)


def end_context_kernel(at_ref, a_ref, b_ref, c_ref, out_ref):
    step = pl.program_id(0)
    rows = pl.ds(pl.multiple_of(step * 128, 128), 128)
    place = pl.ds(pl.multiple_of((step % 2) * 128, 128), 128)

    @pl.when(step < 2)
    def _():
        out_ref[...] = (a_ref[rows, :] + b_ref[place, :].astype(F32)).astype(BF16)

    @pl.when(step >= 2)
    def _():
        out_ref[...] = (a_ref[rows, :] + c_ref[place, :].astype(F32)).astype(BF16)


def end_context(at, own, *got):
    return call(
        end_context_kernel,
        "end_context", 2,
        jax.ShapeDtypeStruct((512, 2048), BF16),
        (4,),
        [HELD, HELD, HELD],
        pl.BlockSpec((128, 2048), lambda i, at: (i, 0)),
    )(at, own, *got)


def place_x_kernel(at_ref, high_ref, low_ref, sent_ref, out_ref, gain_ref):
    step = pl.program_id(0)
    rows = pl.ds(pl.multiple_of((step % 2) * 64, 64), 64)

    @pl.when(step < 2)
    def _():
        out_ref[...] = high_ref[rows, :].astype(F32)

    @pl.when(step >= 2)
    def _():
        out_ref[...] = low_ref[rows, :].astype(F32)

    @pl.when(step == 0)
    def _():
        own = pl.ds(pl.multiple_of(at_ref[8] * HALF, 256), HALF)
        other = pl.ds(pl.multiple_of((1 - at_ref[8]) * HALF, 256), HALF)
        gain_ref[:, own] = one_value(sent_ref[128:])
        gain_ref[:, other] = one_value(low_ref[128:])


def place_x(at, high, low, sent):
    return call(
        place_x_kernel,
        "place_x", 2,
        [jax.ShapeDtypeStruct((256, 2 * HALF), F32), jax.ShapeDtypeStruct((1, 2 * HALF), F32)],
        (4,),
        [HELD, HELD, HELD],
        [
            pl.BlockSpec((64, HALF), lambda i, at: (i, 1 - at[8])),
            pl.BlockSpec((1, 2 * HALF), lambda i, at: (0, 0)),
        ],
    )(at, high, low, sent)


def place_o_kernel(at_ref, out_in_ref, a_ref, b_ref, c_ref, out_ref):
    rows = pl.ds(pl.multiple_of(pl.program_id(0) * 64, 64), 64)
    out_ref[...] = a_ref[rows, :] + b_ref[rows, :].astype(F32) + c_ref[rows, :].astype(F32)


def place_o(at, out, a, b, c):
    return call(
        place_o_kernel,
        "place_o", 2,
        jax.ShapeDtypeStruct((256, 2 * HALF), F32),
        (4,),
        [pl.BlockSpec(memory_space=pl.ANY), HELD, HELD, HELD],
        pl.BlockSpec((64, HALF), lambda i, at: (i, at[8])),
        aliases={1: 0},
    )(at, out, a, b, c)


def per_device(context, cotangent, weight, gain, delta, anchor, momentum):
    r = lax.axis_index("replica")
    z_lo, x, core = r // 8, (r // 2) % 4, r % 2
    f = lax.axis_index("fsdp")
    y, z = f // 2, f % 2
    low, high = y ^ 1, jnp.where(y % 2 == 0, (y + 3) % 4, (y + 1) % 4)
    partner = jnp.where(core == 0, low, high)
    mate = jnp.where(core == 0, high, low)
    opposite = (y + 2) % 4
    half = jnp.where(core == 0, ((y + 1) // 2) % 2, y // 2)

    def numbers(*values):
        return jnp.stack([jnp.asarray(value, jnp.int32) for value in values])

    def place(owner, zz):
        return owner * 2 + zz

    turn_order = numbers(
        place(opposite, 1 - z),
        place(mate, 1 - z),
        place(partner, 1 - z),
        place(mate, z),
        place(opposite, z),
        place(y, 1 - z),
        place(partner, z),
        place(y, z),
    )
    at = numbers(
        place(y, z),
        place(mate, z),
        place(partner, z),
        place(y, 1 - z),
        place(opposite, z),
        place(mate, 1 - z),
        place(partner, 1 - z),
        place(opposite, 1 - z),
        half,
    )
    which, which_core = numbers(half), numbers(core)
    x_away, x_pair = x ^ 1, 3 - x
    x1_at = numbers(
        x_away, 3 - x_away, 4 + x_away, 7 - x_away,
        x, x_pair, 4 + x, 4 + x_pair,
    )
    x3_at = numbers(1, 3, 0, 2)
    zlo_at = numbers(1 - z_lo, z_lo)

    own, other = split(which, weight[0])
    own_z = send(own, TO_Z)
    from_mate = send(own, TO_MATE)

    cot, cot_away = split(which, after(cotangent, own))
    core_low, core_high, core_kept = outer_parts(which_core, after(delta[0], own))
    core_got = [send(core_low, TO_CORE), send(core_high, TO_CORE)]
    from_partner = send(after(other, cot_away, core_high), TO_PARTNER)
    from_mate = after(from_mate, own_z, *core_got)

    mate_z = send(from_mate, TO_Z)
    from_partner = after(from_partner, from_mate)
    from_opposite = send(from_partner, TO_MATE)
    partner_z = send(from_partner, TO_Z)
    context_p = send(after(context, from_partner), TO_PARTNER)
    cot_p = send(after(cot_away, from_partner), TO_PARTNER)
    x1_away, x1_kept = outer_sum(x1_at, after(core_kept, from_partner), *core_got)
    from_opposite = after(from_opposite, mate_z, x1_away)

    x1_got = send(after(x1_away, from_opposite), TO_X1)
    opposite_z = send(from_opposite, TO_Z)

    turned, slab = turn(turn_order, context, context_p)
    x3_away, x3_kept = outer_sum(x3_at, after(x1_kept, turned), x1_got)
    x3_got = send(x3_away, TO_X3)
    blocks = [own, from_mate, from_partner, own_z, from_opposite, mate_z, partner_z, opposite_z]
    acc = project(at, context, after(context_p, turned, x3_away), blocks[:-1])
    zlo_away, zlo_kept = outer_sum(zlo_at, after(x3_kept, acc), x3_got, turned=True)
    zlo_got = send(zlo_away, TO_ZLO)

    last = (at, after(acc, zlo_away), slab, opposite_z, cot, cot_p, gain)
    mine = row_stats(*last)
    theirs = send(mine, TO_PARTNER)

    outer_grad = (after(zlo_kept, mine)[0, :COLS] + zlo_got[0, :COLS].astype(F32)) / 16
    new_momentum = 0.9 * momentum.T + outer_grad
    new_anchor = anchor.T - 0.7 * (outer_grad + 0.9 * new_momentum)
    new_momentum, new_anchor = new_momentum.T, new_anchor.T

    theirs = after(theirs, new_anchor, new_momentum)
    g, x_mate_away, o_mate_z = grad_step(*last, mine, theirs, turned)

    x_mate_z = send(x_mate_away, TO_Z)
    o_mate_z = send(o_mate_z, TO_MATE)
    part_p = context_term(at, g, 512, blocks, BF16, 1)
    got_high = send(part_p, TO_PARTNER)
    x_self_z, o_mate = weight_terms(which, turned, after(g, part_p), 2, 2, BF16)
    x_self_z = send(x_self_z, TO_Z)
    x_mate_own, o_self_z_own, x_self_own, o_self_own = weight_terms(
        which, turned, after(g, o_mate), 4, 4, F32
    )

    part_p = context_term(at, after(g, x_self_own), 768, blocks, BF16, 1)
    got_low = send(part_p, TO_PARTNER)

    x_mate = add_x(which, x_mate_own, x_mate_away, after(x_mate_z, part_p, o_mate_z))
    x_from_mate = [send(piece, TO_MATE) for piece in x_mate]
    o_self_z = add(which, after(o_self_z_own, x_mate[0]), o_mate_z)
    o_from_z = send(o_self_z, TO_Z)
    own_context = context_term(at, after(g, o_self_z), 0, blocks, F32, 2)
    o_mate = send(after(o_mate, x_mate[0], got_high), TO_MATE)

    x_self = add_x(
        which, x_self_own, x_mate[1], after(x_from_mate[0], own_context), x_from_mate[1], x_self_z
    )
    x_got = [send(piece, TO_PARTNER) for piece in x_self]
    grad_context = end_context(which, after(own_context, x_self[0]), got_high, got_low)
    grad_weight, grad_gain = place_x(at, after(x_got[0], grad_context), x_got[1], x_self[1])
    grad_weight = place_o(at, grad_weight, o_self_own, o_mate, o_from_z)
    return (grad_context, grad_weight[None], grad_gain, new_anchor, new_momentum)


def solution(mesh):
    placed = (
        P(("replica", "fsdp"), None),
        P(("replica", "fsdp"), None),
        P("replica", "fsdp", None),
        P("replica", None),
        P("replica", "fsdp", None),
        P("fsdp", "replica"),
        P("fsdp", "replica"),
    )
    return jax.shard_map(
        per_device,
        mesh=mesh,
        in_specs=placed,
        out_specs=(
            P(("replica", "fsdp"), None),
            P("replica", "fsdp", None),
            P("replica", None),
            P("fsdp", "replica"),
            P("fsdp", "replica"),
        ),
        check_vma=False,
    )
```

```python
import jax
import jax.numpy as jnp
from jax import lax
from jax.experimental import pallas as pl
from jax.experimental.pallas import tpu as pltpu
from jax.sharding import PartitionSpec as P

BF16 = jnp.bfloat16
F32 = jnp.float32
BOTH = ("replica", "fsdp")
HALF = 1792
COLS = 224
WIDE = 256
TILE = 256
TILES = HALF // TILE
LIMIT = 10 * 2**20


def partner_y(y, core):
    if core == 0:
        return y ^ 1
    return (y - 1) % 4 if y % 2 == 0 else (y + 1) % 4


def table(move):
    pairs = []
    for r in range(16):
        for f in range(8):
            z_lo, x, core, y, z_hi = r // 8, (r // 2) % 4, r % 2, f // 2, f % 2
            z_lo, x, core, y, z_hi = move(z_lo, x, core, y, z_hi)
            pairs.append((r * 8 + f, ((z_lo * 4 + x) * 2 + core) * 8 + y * 2 + z_hi))
    return pairs


TO_PARTNER = table(lambda a, x, c, y, z: (a, x, c, partner_y(y, c), z))
TO_MATE = table(lambda a, x, c, y, z: (a, x, c, partner_y(y, 1 - c), z))
TO_Z = table(lambda a, x, c, y, z: (a, x, c, y, 1 - z))
TO_CORE = table(lambda a, x, c, y, z: (a, x, 1 - c, y, z))
TO_X1 = table(lambda a, x, c, y, z: (a, x ^ 1, c, y, z))
TO_X3 = table(lambda a, x, c, y, z: (a, 3 - x, c, y, z))
TO_ZLO = table(lambda a, x, c, y, z: (1 - a, x, c, y, z))


def send(value, pairs):
    return lax.ppermute(value, BOTH, pairs)


def after(value, *others):
    return lax.optimization_barrier((value, *others))[0]


HELD = pl.BlockSpec(memory_space=pltpu.VMEM)


def near(x):
    return pltpu.with_memory_space_constraint(x, pltpu.VMEM)


def far(x):
    return pltpu.with_memory_space_constraint(x, pltpu.HBM)


def call(kernel, name, cost, out_shape, grid, in_specs, out_specs, scratch=(), aliases=None):
    built = pl.pallas_call(
        kernel,
        out_shape=out_shape,
        grid_spec=pltpu.PrefetchScalarGridSpec(
            num_scalar_prefetch=1,
            grid=grid,
            in_specs=in_specs,
            out_specs=out_specs,
            scratch_shapes=list(scratch),
        ),
        compiler_params=pltpu.CompilerParams(vmem_limit_bytes=LIMIT),
        cost_estimate=pl.CostEstimate(flops=0, bytes_accessed=int(cost * 3e6), transcendentals=0),
        input_output_aliases=aliases or {},
        name=name,
    )

    def run(at, *operands):
        placed = [near(x) if spec is HELD else far(x) for x, spec in zip(operands, in_specs)]
        return built(at, *placed)

    return run


def split_kernel(at_ref, in_ref, own_ref, other_ref, sems):
    copies = []
    rows = own_ref.shape[0] // 4
    for i in range(4):
        for s, (out_ref, half) in enumerate(((own_ref, at_ref[0]), (other_ref, 1 - at_ref[0]))):
            part = pl.ds(i * rows, rows)
            lanes = pl.ds(pl.multiple_of(half * HALF, 256), HALF)
            copies.append(
                pltpu.make_async_copy(in_ref.at[part, lanes], out_ref.at[part], sems.at[s, i])
            )
    for copy in copies:
        copy.start()
    for copy in copies:
        copy.wait()


def split(which, array):
    return call(
        split_kernel,
        "split", 2,
        [pltpu.VMEM((array.shape[0], HALF), BF16)] * 2,
        (1,),
        [pl.BlockSpec(memory_space=pl.ANY)],
        [HELD] * 2,
        [pltpu.SemaphoreType.DMA((2, 4))],
    )(which, array)


def turn_kernel(at_ref, own_ref, high_ref, low_ref, out_ref, slab_ref):
    pieces = ((own_ref, 0, 512), (high_ref, 512, 768), (low_ref, 768, 1024))
    for ref, start, stop in pieces:
        for k in range(8):
            at = pl.ds(pl.multiple_of(at_ref[k] * 256, 256), 256)
            out_ref[k * 256 : (k + 1) * 256, start:stop] = jnp.transpose(ref[:, at])
        at = pl.ds(pl.multiple_of(at_ref[0] * 256, 256), 256)
        slab_ref[start:stop] = ref[:, at]


def turn(at, context, context_p):
    return call(
        turn_kernel,
        "turn", 4,
        [pltpu.VMEM((2048, 1024), BF16), pltpu.VMEM((1024, 256), BF16)],
        (1,),
        [HELD, HELD, HELD],
        [HELD, HELD],
    )(at, context, *context_p)


def outer_parts_kernel(at_ref, delta_ref, low_ref, high_ref, kept_ref):
    rows = pl.ds(pl.multiple_of(pl.program_id(0) * 64, 64), 64)
    for core in range(2):

        @pl.when(at_ref[0] == core)
        def _(core=core):
            for k in range(8):
                away, kept = (2 * k + 1 - core) * COLS, (2 * k + core) * COLS
                away_ref = low_ref if k < 4 else high_ref
                away_ref[k % 4, rows, :COLS] = delta_ref[:, away : away + COLS].astype(BF16)
                kept_ref[k, rows, :COLS] = delta_ref[:, kept : kept + COLS]


def outer_parts(at, delta):
    return call(
        outer_parts_kernel,
        "outer_parts", 3,
        [pltpu.VMEM((4, 256, WIDE), BF16)] * 2 + [pltpu.VMEM((8, 256, WIDE), F32)],
        (4,),
        [pl.BlockSpec((64, 16 * COLS), lambda i, at: (i, 0))],
        [HELD, HELD, HELD],
    )(at, delta)


def outer_sum_kernel(at_ref, kept_in_ref, *refs, turned):
    *got_refs, away_ref, kept_ref = refs
    n = away_ref.shape[0]
    view = jnp.transpose if turned else lambda block: block

    def total(i, at):
        piece = i * len(got_refs) // n
        got = got_refs[piece][at - piece * got_refs[0].shape[0]]
        return view(kept_in_ref[at] + got.astype(F32))

    for i in range(n):
        away_ref[i] = total(i, at_ref[i]).astype(BF16)
        kept_ref[i] = total(i, at_ref[n + i])


def outer_sum(at, kept, *got, turned=False):
    n = at.shape[0] // 2

    def kernel(*refs):
        outer_sum_kernel(*refs, turned=turned)

    return call(
        kernel,
        "outer_sum", 4,
        [pltpu.VMEM((n, 256, WIDE), BF16), pltpu.VMEM((n, 256, WIDE), F32)],
        (1,),
        [HELD] * (1 + len(got)),
        [HELD, HELD],
    )(at, kept, *got)


def slabs(at_ref, block_refs):
    k = 0
    for ref in block_refs:
        for row in range(0, ref.shape[0], 256):
            yield ref, row, pl.ds(pl.multiple_of(at_ref[k] * 256, 256), 256)
            k += 1


def project_kernel(at_ref, own_ref, high_ref, low_ref, *refs):
    *block_refs, out_ref = refs
    pieces = ((own_ref, 0, 512), (high_ref, 512, 768), (low_ref, 768, 1024))
    for j in range(TILES):
        lanes = slice(j * TILE, (j + 1) * TILE)
        for rows_ref, start, stop in pieces:
            total = None
            for ref, row, at in slabs(at_ref, block_refs):
                term = jnp.dot(
                    rows_ref[:, at], ref[row : row + 256, lanes], preferred_element_type=F32
                )
                total = term if total is None else total + term
            out_ref[start:stop, lanes] = total


def project(at, context, context_p, blocks):
    return call(
        project_kernel,
        "project", 14,
        pltpu.VMEM((1024, HALF), F32),
        (1,),
        [HELD] * (3 + len(blocks)),
        HELD,
    )(at, context, *context_p, *blocks)


def gain_lanes(at_ref, j):
    return pl.ds(pl.multiple_of(at_ref[8] * HALF + j * TILE, TILE), TILE)


def stats_kernel(
    at_ref, acc_ref, slab_ref, block_ref, cot_ref, high_ref, low_ref, gain_ref, out_ref
):
    for s in range(4):
        rows = slice(s * 256, (s + 1) * 256)
        part = rows if s < 2 else slice(None)
        c_ref = (cot_ref, cot_ref, high_ref, low_ref)[s]
        squares = jnp.zeros((256, 128), F32)
        products = jnp.zeros((256, 128), F32)
        for j in range(TILES):
            lanes = slice(j * TILE, (j + 1) * TILE)
            p = acc_ref[rows, lanes] + jnp.dot(
                slab_ref[rows], block_ref[:, lanes], preferred_element_type=F32
            )
            scaled = c_ref[part, lanes].astype(F32) * gain_ref[:, gain_lanes(at_ref, j)] * p
            p = p * p
            squares += p[:, :128] + p[:, 128:]
            products += scaled[:, :128] + scaled[:, 128:]
        for i in range(2):
            chunk = slice(i * 128, (i + 1) * 128)
            top = jnp.sum(jnp.transpose(squares[chunk]), axis=0, keepdims=True)
            low = jnp.sum(jnp.transpose(products[chunk]), axis=0, keepdims=True)
            out_ref[2 * s + i] = jnp.concatenate([top] * 4 + [low] * 4, axis=0)


def row_stats(at, acc, slab, block, cot, cot_p, gain):
    return call(
        stats_kernel,
        "row_stats", 3,
        pltpu.VMEM((8, 8, 128), F32),
        (1,),
        [HELD] * 7,
        HELD,
    )(at, acc, slab, block, cot, *cot_p, gain)


def two_parts(value):
    high = value.astype(BF16).astype(F32)
    row = lax.broadcasted_iota(jnp.int32, (16, value.shape[1]), 0)
    return jnp.where(row == 0, high, jnp.where(row == 1, value - high, 0.0)).astype(BF16)


def one_value(rows):
    return jnp.sum(rows.astype(F32), axis=0, keepdims=True)


def grad_kernel(
    at_ref, acc_ref, slab_ref, block_ref, cot_ref, high_ref, low_ref, gain_ref, mine_ref,
    theirs_ref, turned_ref,
    g_ref, x_mate_ref, o_z_ref, a_ref, b_ref,
):
    for i in range(8):
        total = mine_ref[i] + theirs_ref[(i + 4) % 8]
        inverse = lax.rsqrt(total[0:1] / 3584 + 1e-06)
        coupling = total[4:5] / 3584 * inverse * inverse * inverse
        rows = pl.ds(i * 128, 128)
        a_ref[rows, :] = jnp.transpose(jnp.broadcast_to(inverse, (128, 128)))
        b_ref[rows, :] = jnp.transpose(jnp.broadcast_to(coupling, (128, 128)))

    for j in range(TILES):
        lanes = slice(j * TILE, (j + 1) * TILE)
        block = block_ref[:, lanes]
        gain = gain_ref[:, gain_lanes(at_ref, j)]
        gain_total = jnp.zeros((8, TILE), F32)
        for i in range(4):
            rows = slice(i * 256, (i + 1) * 256)
            part = rows if i < 2 else slice(None)
            c_ref = (cot_ref, cot_ref, high_ref, low_ref)[i]
            p = acc_ref[rows, lanes] + jnp.dot(slab_ref[rows], block, preferred_element_type=F32)
            inverse = jnp.concatenate([a_ref[rows]] * 2, axis=1)
            coupling = jnp.concatenate([b_ref[rows]] * 2, axis=1)
            cot = c_ref[part, lanes].astype(F32) * inverse
            g_ref[rows, lanes] = (cot * gain - p * coupling).astype(BF16)
            gain_total += jnp.sum((cot * p).reshape(32, 8, TILE), axis=0)
        terms = jnp.dot(turned_ref[:512], g_ref[:, lanes], preferred_element_type=F32)
        terms = terms.astype(BF16)
        x_mate_ref[:256, lanes] = terms[:256]
        x_mate_ref[256:, lanes] = two_parts(jnp.sum(gain_total, axis=0, keepdims=True))
        o_z_ref[:, lanes] = terms[256:]


def grad_step(at, acc, slab, block, cot, cot_p, gain, mine, theirs, turned):
    return call(
        grad_kernel,
        "grad_step", 6,
        (
            pltpu.VMEM((1024, HALF), BF16),
            pltpu.VMEM((272, HALF), BF16),
            pltpu.VMEM((256, HALF), BF16),
        ),
        (1,),
        [HELD] * 10,
        [HELD] * 3,
        [pltpu.VMEM((1024, 128), F32), pltpu.VMEM((1024, 128), F32)],
    )(at, acc, slab, block, cot, *cot_p, gain, mine, theirs, turned)


def weight_kernel(at_ref, turned_ref, g_ref, *out_refs, first):
    n = len(out_refs)
    for j in range(TILES):
        lanes = slice(j * TILE, (j + 1) * TILE)
        terms = jnp.dot(
            turned_ref[first * 256 : (first + n) * 256],
            g_ref[:, lanes],
            preferred_element_type=F32,
        )
        for k, out_ref in enumerate(out_refs):
            out_ref[:, lanes] = terms[k * 256 : (k + 1) * 256].astype(out_ref.dtype)


def weight_terms(at, turned, g, first, n, dtype):
    def kernel(*refs):
        weight_kernel(*refs, first=first)

    return call(
        kernel,
        "weight_terms", n,
        [pltpu.VMEM((256, HALF), dtype)] * n,
        (1,),
        [HELD, HELD],
        [HELD] * n,
    )(at, turned, g)


def context_kernel(at_ref, g_ref, *refs, first):
    *block_refs, out_ref = refs
    rows = slice(first, first + out_ref.shape[0])
    for ref, row, at in slabs(at_ref, block_refs):
        part = lax.dot_general(
            g_ref[rows, :],
            ref[row : row + 256],
            (((1,), (1,)), ((), ())),
            preferred_element_type=F32,
        )
        out_ref[:, at] = part.astype(out_ref.dtype)


def context_term(at, g, first, blocks, dtype, tiles):
    def kernel(*refs):
        context_kernel(*refs, first=first)

    return call(
        kernel,
        "context_term", 2.5 * tiles,
        pltpu.VMEM((256 * tiles, 2048), dtype),
        (1,),
        [HELD] * (1 + len(blocks)),
        HELD,
    )(at, g, *blocks)


def add_kernel(at_ref, a_ref, b_ref, out_ref):
    out_ref[...] = (a_ref[...] + b_ref[...].astype(F32)).astype(BF16)


def add(at, a, b):
    return call(
        add_kernel, "add", 1, pltpu.VMEM((256, HALF), BF16), (1,), [HELD, HELD], HELD
    )(at, a, b)


def add_x_kernel(at_ref, a_ref, *refs):
    *in_refs, high_ref, low_ref = refs
    sent_ref, *got_refs = in_refs
    total = a_ref[...]
    if got_refs[0].shape[0] == 128:
        got = jnp.concatenate([got_refs[0][...], got_refs[1][:128]], axis=0)
        sums_ref, more = got_refs[1], got_refs[2:]
    else:
        got = got_refs[0][:256]
        sums_ref, more = got_refs[0], got_refs[1:]
    total = total + got.astype(F32)
    for ref in more:
        total = total + ref[...].astype(F32)
    high_ref[...] = total[:128].astype(BF16)
    low_ref[:128] = total[128:].astype(BF16)
    sums = one_value(sent_ref[sent_ref.shape[0] - 16 :])
    low_ref[128:] = two_parts(sums + one_value(sums_ref[sums_ref.shape[0] - 16 :]))


def add_x(at, own, sent, *got):
    return call(
        add_x_kernel,
        "add_x", 1,
        [pltpu.VMEM((128, HALF), BF16), pltpu.VMEM((144, HALF), BF16)],
        (1,),
        [HELD] * (2 + len(got)),
        [HELD, HELD],
    )(at, own, sent, *got)


def end_context_kernel(at_ref, a_ref, b_ref, c_ref, out_ref):
    step = pl.program_id(0)
    rows = pl.ds(pl.multiple_of(step * 128, 128), 128)
    place = pl.ds(pl.multiple_of((step % 2) * 128, 128), 128)

    @pl.when(step < 2)
    def _():
        out_ref[...] = (a_ref[rows, :] + b_ref[place, :].astype(F32)).astype(BF16)

    @pl.when(step >= 2)
    def _():
        out_ref[...] = (a_ref[rows, :] + c_ref[place, :].astype(F32)).astype(BF16)


def end_context(at, own, *got):
    return call(
        end_context_kernel,
        "end_context", 2,
        jax.ShapeDtypeStruct((512, 2048), BF16),
        (4,),
        [HELD, HELD, HELD],
        pl.BlockSpec((128, 2048), lambda i, at: (i, 0)),
    )(at, own, *got)


def finish_kernel(
    at_ref, high_ref, low_ref, sent_ref, o_ref, o_mate_ref, o_z_ref,
    out_ref, gain_ref, own_stage, other_stage, sems,
):
    own = pl.ds(pl.multiple_of(at_ref[8] * HALF, 256), HALF)
    other = pl.ds(pl.multiple_of((1 - at_ref[8]) * HALF, 256), HALF)
    copies = []
    for i in range(4):
        rows = slice(i * 64, (i + 1) * 64)
        x_ref, part = (high_ref, rows) if i < 2 else (low_ref, slice(i * 64 - 128, i * 64 - 64))
        other_stage[rows] = x_ref[part].astype(F32)
        own_stage[rows] = (
            o_ref[rows] + o_mate_ref[rows].astype(F32) + o_z_ref[rows].astype(F32)
        )
        for s, (stage, lanes) in enumerate(((other_stage, other), (own_stage, own))):
            part = pl.ds(i * 64, 64)
            copies.append(
                pltpu.make_async_copy(stage.at[part], out_ref.at[part, lanes], sems.at[s, i])
            )
            copies[-1].start()
    gain_ref[:, own] = one_value(sent_ref[128:])
    gain_ref[:, other] = one_value(low_ref[128:])
    for copy in copies:
        copy.wait()


def finish(at, high, low, sent, o, o_mate, o_z):
    return call(
        finish_kernel,
        "finish", 2,
        [jax.ShapeDtypeStruct((256, 2 * HALF), F32), jax.ShapeDtypeStruct((1, 2 * HALF), F32)],
        (1,),
        [HELD] * 6,
        [
            pl.BlockSpec(memory_space=pl.ANY),
            pl.BlockSpec((1, 2 * HALF), lambda i, at: (0, 0)),
        ],
        [
            pltpu.VMEM((256, HALF), F32),
            pltpu.VMEM((256, HALF), F32),
            pltpu.SemaphoreType.DMA((2, 4)),
        ],
    )(at, high, low, sent, o, o_mate, o_z)


def per_device(context, cotangent, weight, gain, delta, anchor, momentum):
    r = lax.axis_index("replica")
    z_lo, x, core = r // 8, (r // 2) % 4, r % 2
    f = lax.axis_index("fsdp")
    y, z = f // 2, f % 2
    low, high = y ^ 1, jnp.where(y % 2 == 0, (y + 3) % 4, (y + 1) % 4)
    partner = jnp.where(core == 0, low, high)
    mate = jnp.where(core == 0, high, low)
    opposite = (y + 2) % 4
    half = jnp.where(core == 0, ((y + 1) // 2) % 2, y // 2)

    def numbers(*values):
        return jnp.stack([jnp.asarray(value, jnp.int32) for value in values])

    def place(owner, zz):
        return owner * 2 + zz

    turn_order = numbers(
        place(opposite, 1 - z),
        place(mate, 1 - z),
        place(partner, 1 - z),
        place(mate, z),
        place(opposite, z),
        place(y, 1 - z),
        place(partner, z),
        place(y, z),
    )
    at = numbers(
        place(y, z),
        place(mate, z),
        place(partner, z),
        place(y, 1 - z),
        place(opposite, z),
        place(mate, 1 - z),
        place(partner, 1 - z),
        place(opposite, 1 - z),
        half,
    )
    which, which_core = numbers(half), numbers(core)
    x_away, x_pair = x ^ 1, 3 - x
    x1_at = numbers(
        x_away, 3 - x_away, 4 + x_away, 7 - x_away,
        x, x_pair, 4 + x, 4 + x_pair,
    )
    x3_at = numbers(1, 3, 0, 2)
    zlo_at = numbers(1 - z_lo, z_lo)

    own, other = split(which, weight[0])
    own_z = send(own, TO_Z)
    from_mate = send(own, TO_MATE)

    cot, cot_away = split(which, after(cotangent, own))
    core_low, core_high, core_kept = outer_parts(which_core, after(delta[0], own))
    core_got = [send(core_low, TO_CORE), send(core_high, TO_CORE)]
    from_partner = send(after(other, cot_away, core_high), TO_PARTNER)
    from_mate = after(from_mate, own_z, *core_got)

    mate_z = send(from_mate, TO_Z)
    from_partner = after(from_partner, from_mate)
    from_opposite = send(from_partner, TO_MATE)
    partner_z = send(from_partner, TO_Z)
    context_p = [
        send(after(context[:256], core_high), TO_PARTNER),
        send(after(context[256:], core_high), TO_PARTNER),
    ]
    x1_away, x1_kept = outer_sum(x1_at, after(core_kept, from_partner, mate_z), *core_got)
    from_opposite = after(from_opposite, mate_z, x1_away, context_p[0])

    x1_got = send(after(x1_away, from_opposite), TO_X1)
    opposite_z = send(from_opposite, TO_Z)
    cot_p = [
        send(after(cot_away[:256], from_opposite), TO_PARTNER),
        send(after(cot_away[256:], from_opposite), TO_PARTNER),
    ]

    turned, slab = turn(turn_order, context, context_p)
    blocks = [own, from_mate, from_partner, own_z, from_opposite, mate_z, partner_z, opposite_z]
    acc = project(at, after(context, turned), context_p, blocks[:-1])
    last = (at, acc, slab, opposite_z, cot, cot_p, gain)
    mine = row_stats(*last)
    theirs = send(mine, TO_PARTNER)
    x3_away, x3_kept = outer_sum(x3_at, after(x1_kept, mine), x1_got)
    theirs = after(theirs, x3_away)
    g, x_mate_away, o_mate_z = grad_step(*last, mine, theirs, turned)

    x_mate_z = send(x_mate_away, TO_Z)
    o_mate_z = send(o_mate_z, TO_MATE)
    part_p = context_term(at, g, 512, blocks, BF16, 1)
    got_high = send(part_p, TO_PARTNER)
    x_self_z, o_mate = weight_terms(which, turned, after(g, part_p), 2, 2, BF16)
    x_self_z = send(x_self_z, TO_Z)
    x_mate_own, o_self_z_own, x_self_own, o_self_own = weight_terms(
        which, turned, after(g, o_mate), 4, 4, F32
    )

    part_p = context_term(at, after(g, x_self_own), 768, blocks, BF16, 1)
    got_low = send(part_p, TO_PARTNER)

    x_mate = add_x(which, x_mate_own, x_mate_away, after(x_mate_z, part_p, o_mate_z))
    x_from_mate = [send(piece, TO_MATE) for piece in x_mate]
    o_self_z = add(which, after(o_self_z_own, x_mate[0]), o_mate_z)
    o_from_z = send(o_self_z, TO_Z)
    x3_got = send(x3_away, TO_X3)
    zlo_away, zlo_kept = outer_sum(zlo_at, after(x3_kept, o_self_z), x3_got, turned=True)
    zlo_got = send(zlo_away, TO_ZLO)
    own_context = context_term(at, after(g, zlo_away), 0, blocks, F32, 2)
    o_mate = send(after(o_mate, x_mate[0], got_high), TO_MATE)

    x_self = add_x(
        which,
        x_self_own,
        x_mate[1],
        after(x_from_mate[0], own_context),
        x_from_mate[1],
        x_self_z,
    )
    x_got = [send(piece, TO_PARTNER) for piece in x_self]
    grad_context = end_context(which, after(own_context, x_self[0]), got_high, got_low)
    outer_grad = (after(zlo_kept, grad_context)[0, :COLS] + zlo_got[0, :COLS].astype(F32)) / 16
    new_momentum = 0.9 * momentum.T + outer_grad
    new_anchor = anchor.T - 0.7 * (outer_grad + 0.9 * new_momentum)
    new_momentum, new_anchor = new_momentum.T, new_anchor.T
    grad_weight, grad_gain = finish(
        at, after(x_got[0], new_anchor, new_momentum), x_got[1], x_self[1], o_self_own, o_mate, o_from_z
    )
    return (grad_context, grad_weight[None], grad_gain, new_anchor, new_momentum)


def solution(mesh):
    placed = (
        P(("replica", "fsdp"), None),
        P(("replica", "fsdp"), None),
        P("replica", "fsdp", None),
        P("replica", None),
        P("replica", "fsdp", None),
        P("fsdp", "replica"),
        P("fsdp", "replica"),
    )
    return jax.shard_map(
        per_device,
        mesh=mesh,
        in_specs=placed,
        out_specs=(
            P(("replica", "fsdp"), None),
            P("replica", "fsdp", None),
            P("replica", None),
            P("fsdp", "replica"),
            P("fsdp", "replica"),
        ),
        check_vma=False,
    )
```

```python
import jax
import jax.numpy as jnp
from jax import lax
from jax.experimental import pallas as pl
from jax.experimental.pallas import tpu as pltpu
from jax.sharding import PartitionSpec as P

BF16 = jnp.bfloat16
F32 = jnp.float32
BOTH = ("replica", "fsdp")
HALF = 1792
COLS = 224
WIDE = 256
TILE = 256
TILES = HALF // TILE
LIMIT = 10 * 2**20


def partner_y(y, core):
    if core == 0:
        return y ^ 1
    return (y - 1) % 4 if y % 2 == 0 else (y + 1) % 4


def table(move):
    pairs = []
    for r in range(16):
        for f in range(8):
            z_lo, x, core, y, z_hi = r // 8, (r // 2) % 4, r % 2, f // 2, f % 2
            z_lo, x, core, y, z_hi = move(z_lo, x, core, y, z_hi)
            pairs.append((r * 8 + f, ((z_lo * 4 + x) * 2 + core) * 8 + y * 2 + z_hi))
    return pairs


TO_PARTNER = table(lambda a, x, c, y, z: (a, x, c, partner_y(y, c), z))
TO_MATE = table(lambda a, x, c, y, z: (a, x, c, partner_y(y, 1 - c), z))
TO_Z = table(lambda a, x, c, y, z: (a, x, c, y, 1 - z))
TO_CORE = table(lambda a, x, c, y, z: (a, x, 1 - c, y, z))
TO_X1 = table(lambda a, x, c, y, z: (a, x ^ 1, c, y, z))
TO_X3 = table(lambda a, x, c, y, z: (a, 3 - x, c, y, z))
TO_ZLO = table(lambda a, x, c, y, z: (1 - a, x, c, y, z))


def send(value, pairs):
    return lax.ppermute(value, BOTH, pairs)


def after(value, *others):
    return lax.optimization_barrier((value, *others))[0]


HELD = pl.BlockSpec(memory_space=pltpu.VMEM)


def near(x):
    return pltpu.with_memory_space_constraint(x, pltpu.VMEM)


def far(x):
    return pltpu.with_memory_space_constraint(x, pltpu.HBM)


def call(kernel, name, cost, out_shape, grid, in_specs, out_specs, scratch=(), aliases=None):
    built = pl.pallas_call(
        kernel,
        out_shape=out_shape,
        grid_spec=pltpu.PrefetchScalarGridSpec(
            num_scalar_prefetch=1,
            grid=grid,
            in_specs=in_specs,
            out_specs=out_specs,
            scratch_shapes=list(scratch),
        ),
        compiler_params=pltpu.CompilerParams(vmem_limit_bytes=LIMIT),
        cost_estimate=pl.CostEstimate(flops=0, bytes_accessed=int(cost * 3e6), transcendentals=0),
        input_output_aliases=aliases or {},
        name=name,
    )

    def run(at, *operands):
        placed = [near(x) if spec is HELD else far(x) for x, spec in zip(operands, in_specs)]
        return built(at, *placed)

    return run


def split_kernel(at_ref, in_ref, own_ref, other_ref, sems):
    copies = []
    rows = own_ref.shape[0] // 4
    for i in range(4):
        for s, (out_ref, half) in enumerate(((own_ref, at_ref[0]), (other_ref, 1 - at_ref[0]))):
            part = pl.ds(i * rows, rows)
            lanes = pl.ds(pl.multiple_of(half * HALF, 256), HALF)
            copies.append(
                pltpu.make_async_copy(in_ref.at[part, lanes], out_ref.at[part], sems.at[s, i])
            )
    for copy in copies:
        copy.start()
    for copy in copies:
        copy.wait()


def split(which, array):
    return call(
        split_kernel,
        "split", 2,
        [pltpu.VMEM((array.shape[0], HALF), BF16)] * 2,
        (1,),
        [pl.BlockSpec(memory_space=pl.ANY)],
        [HELD] * 2,
        [pltpu.SemaphoreType.DMA((2, 4))],
    )(which, array)


def turn_kernel(at_ref, own_ref, high_ref, low_ref, out_ref, slab_ref):
    pieces = ((own_ref, 0, 512), (high_ref, 512, 768), (low_ref, 768, 1024))
    for ref, start, stop in pieces:
        for k in range(8):
            at = pl.ds(pl.multiple_of(at_ref[k] * 256, 256), 256)
            out_ref[k * 256 : (k + 1) * 256, start:stop] = jnp.transpose(ref[:, at])
        at = pl.ds(pl.multiple_of(at_ref[0] * 256, 256), 256)
        slab_ref[start:stop] = ref[:, at]


def turn(at, context, context_p):
    return call(
        turn_kernel,
        "turn", 4,
        [pltpu.VMEM((2048, 1024), BF16), pltpu.VMEM((1024, 256), BF16)],
        (1,),
        [HELD, HELD, HELD],
        [HELD, HELD],
    )(at, context, *context_p)


def outer_parts_kernel(at_ref, delta_ref, low_ref, high_ref, kept_ref):
    rows = pl.ds(pl.multiple_of(pl.program_id(0) * 64, 64), 64)
    for core in range(2):

        @pl.when(at_ref[0] == core)
        def _(core=core):
            for k in range(8):
                away, kept = (2 * k + 1 - core) * COLS, (2 * k + core) * COLS
                away_ref = low_ref if k < 4 else high_ref
                away_ref[k % 4, rows, :COLS] = delta_ref[:, away : away + COLS].astype(BF16)
                kept_ref[k, rows, :COLS] = delta_ref[:, kept : kept + COLS]


def outer_parts(at, delta):
    return call(
        outer_parts_kernel,
        "outer_parts", 3,
        [pltpu.VMEM((4, 256, WIDE), BF16)] * 2 + [pltpu.VMEM((8, 256, WIDE), F32)],
        (4,),
        [pl.BlockSpec((64, 16 * COLS), lambda i, at: (i, 0))],
        [HELD, HELD, HELD],
    )(at, delta)


def outer_sum_kernel(at_ref, kept_in_ref, *refs, turned):
    *got_refs, away_ref, kept_ref = refs
    n = away_ref.shape[0]
    view = jnp.transpose if turned else lambda block: block

    def total(i, at):
        piece = i * len(got_refs) // n
        got = got_refs[piece][at - piece * got_refs[0].shape[0]]
        return view(kept_in_ref[at] + got.astype(F32))

    for i in range(n):
        away_ref[i] = total(i, at_ref[i]).astype(BF16)
        kept_ref[i] = total(i, at_ref[n + i])


def outer_sum(at, kept, *got, turned=False):
    n = at.shape[0] // 2

    def kernel(*refs):
        outer_sum_kernel(*refs, turned=turned)

    return call(
        kernel,
        "outer_sum", 4,
        [pltpu.VMEM((n, 256, WIDE), BF16), pltpu.VMEM((n, 256, WIDE), F32)],
        (1,),
        [HELD] * (1 + len(got)),
        [HELD, HELD],
    )(at, kept, *got)


def slabs(at_ref, block_refs):
    k = 0
    for ref in block_refs:
        for row in range(0, ref.shape[0], 256):
            yield ref, row, pl.ds(pl.multiple_of(at_ref[k] * 256, 256), 256)
            k += 1


def project_kernel(at_ref, own_ref, high_ref, low_ref, *refs):
    *block_refs, out_ref = refs
    pieces = ((own_ref, 0, 512), (high_ref, 512, 768), (low_ref, 768, 1024))
    for j in range(TILES):
        lanes = slice(j * TILE, (j + 1) * TILE)
        for rows_ref, start, stop in pieces:
            total = None
            for ref, row, at in slabs(at_ref, block_refs):
                term = jnp.dot(
                    rows_ref[:, at], ref[row : row + 256, lanes], preferred_element_type=F32
                )
                total = term if total is None else total + term
            out_ref[start:stop, lanes] = total


def project(at, context, context_p, blocks):
    return call(
        project_kernel,
        "project", 14,
        pltpu.VMEM((1024, HALF), F32),
        (1,),
        [HELD] * (3 + len(blocks)),
        HELD,
    )(at, context, *context_p, *blocks)


def gain_lanes(at_ref, j):
    return pl.ds(pl.multiple_of(at_ref[8] * HALF + j * TILE, TILE), TILE)


def stats_kernel(
    at_ref, acc_ref, slab_ref, block_ref, cot_ref, high_ref, low_ref, gain_ref, out_ref
):
    for s in range(4):
        rows = slice(s * 256, (s + 1) * 256)
        part = rows if s < 2 else slice(None)
        c_ref = (cot_ref, cot_ref, high_ref, low_ref)[s]
        squares = jnp.zeros((256, 128), F32)
        products = jnp.zeros((256, 128), F32)
        for j in range(TILES):
            lanes = slice(j * TILE, (j + 1) * TILE)
            p = acc_ref[rows, lanes] + jnp.dot(
                slab_ref[rows], block_ref[:, lanes], preferred_element_type=F32
            )
            scaled = c_ref[part, lanes].astype(F32) * gain_ref[:, gain_lanes(at_ref, j)] * p
            p = p * p
            squares += p[:, :128] + p[:, 128:]
            products += scaled[:, :128] + scaled[:, 128:]
        for i in range(2):
            chunk = slice(i * 128, (i + 1) * 128)
            top = jnp.sum(jnp.transpose(squares[chunk]), axis=0, keepdims=True)
            low = jnp.sum(jnp.transpose(products[chunk]), axis=0, keepdims=True)
            out_ref[2 * s + i] = jnp.concatenate([top] * 4 + [low] * 4, axis=0)


def row_stats(at, acc, slab, block, cot, cot_p, gain):
    return call(
        stats_kernel,
        "row_stats", 3,
        pltpu.VMEM((8, 8, 128), F32),
        (1,),
        [HELD] * 7,
        HELD,
    )(at, acc, slab, block, cot, *cot_p, gain)


def two_parts(value):
    high = value.astype(BF16).astype(F32)
    row = lax.broadcasted_iota(jnp.int32, (16, value.shape[1]), 0)
    return jnp.where(row == 0, high, jnp.where(row == 1, value - high, 0.0)).astype(BF16)


def one_value(rows):
    return jnp.sum(rows.astype(F32), axis=0, keepdims=True)


def grad_kernel(
    at_ref, acc_ref, slab_ref, block_ref, cot_ref, high_ref, low_ref, gain_ref, mine_ref,
    theirs_ref, turned_ref,
    g_ref, x_mate_ref, o_z_ref, a_ref, b_ref,
):
    for i in range(8):
        total = mine_ref[i] + theirs_ref[(i + 4) % 8]
        inverse = lax.rsqrt(total[0:1] / 3584 + 1e-06)
        coupling = total[4:5] / 3584 * inverse * inverse * inverse
        rows = pl.ds(i * 128, 128)
        a_ref[rows, :] = jnp.transpose(jnp.broadcast_to(inverse, (128, 128)))
        b_ref[rows, :] = jnp.transpose(jnp.broadcast_to(coupling, (128, 128)))

    for j in range(TILES):
        lanes = slice(j * TILE, (j + 1) * TILE)
        block = block_ref[:, lanes]
        gain = gain_ref[:, gain_lanes(at_ref, j)]
        gain_total = jnp.zeros((8, TILE), F32)
        for i in range(4):
            rows = slice(i * 256, (i + 1) * 256)
            part = rows if i < 2 else slice(None)
            c_ref = (cot_ref, cot_ref, high_ref, low_ref)[i]
            p = acc_ref[rows, lanes] + jnp.dot(slab_ref[rows], block, preferred_element_type=F32)
            inverse = jnp.concatenate([a_ref[rows]] * 2, axis=1)
            coupling = jnp.concatenate([b_ref[rows]] * 2, axis=1)
            cot = c_ref[part, lanes].astype(F32) * inverse
            g_ref[rows, lanes] = (cot * gain - p * coupling).astype(BF16)
            gain_total += jnp.sum((cot * p).reshape(32, 8, TILE), axis=0)
        terms = jnp.dot(turned_ref[:512], g_ref[:, lanes], preferred_element_type=F32)
        terms = terms.astype(BF16)
        x_mate_ref[:256, lanes] = terms[:256]
        x_mate_ref[256:, lanes] = two_parts(jnp.sum(gain_total, axis=0, keepdims=True))
        o_z_ref[:, lanes] = terms[256:]


def grad_step(at, acc, slab, block, cot, cot_p, gain, mine, theirs, turned):
    return call(
        grad_kernel,
        "grad_step", 6,
        (
            pltpu.VMEM((1024, HALF), BF16),
            pltpu.VMEM((272, HALF), BF16),
            pltpu.VMEM((256, HALF), BF16),
        ),
        (1,),
        [HELD] * 10,
        [HELD] * 3,
        [pltpu.VMEM((1024, 128), F32), pltpu.VMEM((1024, 128), F32)],
    )(at, acc, slab, block, cot, *cot_p, gain, mine, theirs, turned)


def weight_kernel(at_ref, turned_ref, g_ref, *out_refs, first):
    n = len(out_refs)
    for j in range(TILES):
        lanes = slice(j * TILE, (j + 1) * TILE)
        terms = jnp.dot(
            turned_ref[first * 256 : (first + n) * 256],
            g_ref[:, lanes],
            preferred_element_type=F32,
        )
        for k, out_ref in enumerate(out_refs):
            out_ref[:, lanes] = terms[k * 256 : (k + 1) * 256].astype(out_ref.dtype)


def weight_terms(at, turned, g, first, n, dtype):
    def kernel(*refs):
        weight_kernel(*refs, first=first)

    return call(
        kernel,
        "weight_terms", n,
        [pltpu.VMEM((256, HALF), dtype)] * n,
        (1,),
        [HELD, HELD],
        [HELD] * n,
    )(at, turned, g)


def context_kernel(at_ref, g_ref, *refs, first):
    *block_refs, out_ref = refs
    rows = slice(first, first + out_ref.shape[0])
    for ref, row, at in slabs(at_ref, block_refs):
        part = lax.dot_general(
            g_ref[rows, :],
            ref[row : row + 256],
            (((1,), (1,)), ((), ())),
            preferred_element_type=F32,
        )
        out_ref[:, at] = part.astype(out_ref.dtype)


def context_term(at, g, first, blocks, dtype, tiles):
    def kernel(*refs):
        context_kernel(*refs, first=first)

    return call(
        kernel,
        "context_term", 2.5 * tiles,
        pltpu.VMEM((256 * tiles, 2048), dtype),
        (1,),
        [HELD] * (1 + len(blocks)),
        HELD,
    )(at, g, *blocks)


def add_kernel(at_ref, a_ref, b_ref, out_ref):
    out_ref[...] = (a_ref[...] + b_ref[...].astype(F32)).astype(BF16)


def add(at, a, b):
    return call(
        add_kernel, "add", 1, pltpu.VMEM((256, HALF), BF16), (1,), [HELD, HELD], HELD
    )(at, a, b)


def add_x_kernel(at_ref, a_ref, *refs):
    *in_refs, high_ref, low_ref = refs
    sent_ref, *got_refs = in_refs
    total = a_ref[...]
    if got_refs[0].shape[0] == 128:
        got = jnp.concatenate([got_refs[0][...], got_refs[1][:128]], axis=0)
        sums_ref, more = got_refs[1], got_refs[2:]
    else:
        got = got_refs[0][:256]
        sums_ref, more = got_refs[0], got_refs[1:]
    total = total + got.astype(F32)
    for ref in more:
        total = total + ref[...].astype(F32)
    high_ref[...] = total[:128].astype(BF16)
    low_ref[:128] = total[128:].astype(BF16)
    sums = one_value(sent_ref[sent_ref.shape[0] - 16 :])
    low_ref[128:] = two_parts(sums + one_value(sums_ref[sums_ref.shape[0] - 16 :]))


def add_x(at, own, sent, *got):
    return call(
        add_x_kernel,
        "add_x", 1,
        [pltpu.VMEM((128, HALF), BF16), pltpu.VMEM((144, HALF), BF16)],
        (1,),
        [HELD] * (2 + len(got)),
        [HELD, HELD],
    )(at, own, sent, *got)


def end_context_kernel(at_ref, a_ref, b_ref, c_ref, out_ref):
    step = pl.program_id(0)
    rows = pl.ds(pl.multiple_of(step * 128, 128), 128)
    place = pl.ds(pl.multiple_of((step % 2) * 128, 128), 128)

    @pl.when(step < 2)
    def _():
        out_ref[...] = (a_ref[rows, :] + b_ref[place, :].astype(F32)).astype(BF16)

    @pl.when(step >= 2)
    def _():
        out_ref[...] = (a_ref[rows, :] + c_ref[place, :].astype(F32)).astype(BF16)


def end_context(at, own, *got):
    return call(
        end_context_kernel,
        "end_context", 2,
        jax.ShapeDtypeStruct((512, 2048), BF16),
        (4,),
        [HELD, HELD, HELD],
        pl.BlockSpec((128, 2048), lambda i, at: (i, 0)),
    )(at, own, *got)


def finish_kernel(
    at_ref, high_ref, low_ref, sent_ref, o_ref, o_mate_ref, o_z_ref,
    out_ref, gain_ref, own_stage, other_stage, sems,
):
    own = pl.ds(pl.multiple_of(at_ref[8] * HALF, 256), HALF)
    other = pl.ds(pl.multiple_of((1 - at_ref[8]) * HALF, 256), HALF)
    copies = []
    for i in range(4):
        rows = slice(i * 64, (i + 1) * 64)
        x_ref, part = (high_ref, rows) if i < 2 else (low_ref, slice(i * 64 - 128, i * 64 - 64))
        other_stage[rows] = x_ref[part].astype(F32)
        own_stage[rows] = (
            o_ref[rows] + o_mate_ref[rows].astype(F32) + o_z_ref[rows].astype(F32)
        )
        for s, (stage, lanes) in enumerate(((other_stage, other), (own_stage, own))):
            part = pl.ds(i * 64, 64)
            copies.append(
                pltpu.make_async_copy(stage.at[part], out_ref.at[part, lanes], sems.at[s, i])
            )
            copies[-1].start()
    gain_ref[:, own] = one_value(sent_ref[128:])
    gain_ref[:, other] = one_value(low_ref[128:])
    for copy in copies:
        copy.wait()


def finish(at, high, low, sent, o, o_mate, o_z):
    return call(
        finish_kernel,
        "finish", 2,
        [jax.ShapeDtypeStruct((256, 2 * HALF), F32), jax.ShapeDtypeStruct((1, 2 * HALF), F32)],
        (1,),
        [HELD] * 6,
        [
            pl.BlockSpec(memory_space=pl.ANY),
            pl.BlockSpec((1, 2 * HALF), lambda i, at: (0, 0)),
        ],
        [
            pltpu.VMEM((256, HALF), F32),
            pltpu.VMEM((256, HALF), F32),
            pltpu.SemaphoreType.DMA((2, 4)),
        ],
    )(at, high, low, sent, o, o_mate, o_z)


def per_device(context, cotangent, weight, gain, delta, anchor, momentum):
    r = lax.axis_index("replica")
    z_lo, x, core = r // 8, (r // 2) % 4, r % 2
    f = lax.axis_index("fsdp")
    y, z = f // 2, f % 2
    low, high = y ^ 1, jnp.where(y % 2 == 0, (y + 3) % 4, (y + 1) % 4)
    partner = jnp.where(core == 0, low, high)
    mate = jnp.where(core == 0, high, low)
    opposite = (y + 2) % 4
    half = jnp.where(core == 0, ((y + 1) // 2) % 2, y // 2)

    def numbers(*values):
        return jnp.stack([jnp.asarray(value, jnp.int32) for value in values])

    def place(owner, zz):
        return owner * 2 + zz

    turn_order = numbers(
        place(opposite, 1 - z),
        place(mate, 1 - z),
        place(partner, 1 - z),
        place(mate, z),
        place(opposite, z),
        place(y, 1 - z),
        place(partner, z),
        place(y, z),
    )
    at = numbers(
        place(y, z),
        place(mate, z),
        place(partner, z),
        place(y, 1 - z),
        place(opposite, z),
        place(mate, 1 - z),
        place(partner, 1 - z),
        place(opposite, 1 - z),
        half,
    )
    which, which_core = numbers(half), numbers(core)
    x_away, x_pair = x ^ 1, 3 - x
    x1_at = numbers(
        x_away, 3 - x_away, 4 + x_away, 7 - x_away,
        x, x_pair, 4 + x, 4 + x_pair,
    )
    x3_at = numbers(1, 3, 0, 2)
    zlo_at = numbers(1 - z_lo, z_lo)

    own, other = split(which, weight[0])
    own_z = send(own, TO_Z)
    from_mate = send(own, TO_MATE)

    cot, cot_away = split(which, after(cotangent, own))
    core_low, core_high, core_kept = outer_parts(which_core, after(delta[0], own))
    core_got = [send(core_low, TO_CORE), send(core_high, TO_CORE)]
    from_partner = send(after(other, cot_away, core_high), TO_PARTNER)
    from_mate = after(from_mate, own_z, *core_got)

    mate_z = send(from_mate, TO_Z)
    from_partner = after(from_partner, from_mate)
    from_opposite = send(from_partner, TO_MATE)
    partner_z = send(from_partner, TO_Z)
    context_p = [
        send(after(context[:256], core_high), TO_PARTNER),
        send(after(context[256:], core_high), TO_PARTNER),
    ]
    x1_away, x1_kept = outer_sum(x1_at, after(core_kept, from_partner, mate_z), *core_got)
    from_opposite = after(from_opposite, mate_z, x1_away, context_p[0])

    x1_got = send(after(x1_away, from_opposite), TO_X1)
    opposite_z = send(from_opposite, TO_Z)
    cot_p = [
        send(after(cot_away[:256], from_opposite), TO_PARTNER),
        send(after(cot_away[256:], from_opposite), TO_PARTNER),
    ]

    turned, slab = turn(turn_order, context, context_p)
    blocks = [own, from_mate, from_partner, own_z, from_opposite, mate_z, partner_z, opposite_z]
    acc = project(at, after(context, turned), context_p, blocks[:-1])
    last = (at, acc, slab, opposite_z, cot, cot_p, gain)
    mine = row_stats(*last)
    theirs = send(mine, TO_PARTNER)
    x3_away, x3_kept = outer_sum(x3_at, after(x1_kept, mine), x1_got)
    theirs = after(theirs, x3_away)
    g, x_mate_away, o_mate_z = grad_step(*last, mine, theirs, turned)

    x_mate_z = send(x_mate_away, TO_Z)
    o_mate_z = send(o_mate_z, TO_MATE)
    part_p = context_term(at, g, 512, blocks, BF16, 1)
    got_high = send(part_p, TO_PARTNER)
    x_self_z, o_mate = weight_terms(which, turned, after(g, part_p), 2, 2, BF16)
    x_self_z = send(x_self_z, TO_Z)
    x_mate_own, o_self_z_own, x_self_own, o_self_own = weight_terms(
        which, turned, after(g, o_mate), 4, 4, F32
    )

    part_p = context_term(at, after(g, x_self_own), 768, blocks, BF16, 1)
    got_low = send(part_p, TO_PARTNER)

    x_mate = add_x(which, x_mate_own, x_mate_away, after(x_mate_z, part_p, o_mate_z))
    x_from_mate = [send(piece, TO_MATE) for piece in x_mate]
    o_self_z = add(which, after(o_self_z_own, x_mate[0]), o_mate_z)
    o_from_z = send(o_self_z, TO_Z)
    x3_got = send(x3_away, TO_X3)
    zlo_away, zlo_kept = outer_sum(zlo_at, after(x3_kept, o_self_z), x3_got, turned=True)
    zlo_got = send(zlo_away, TO_ZLO)
    o_mate = send(after(o_mate, x_mate[0], got_high), TO_MATE)

    x_self = add_x(
        which,
        x_self_own,
        x_mate[1],
        after(x_from_mate[0], zlo_away),
        x_from_mate[1],
        x_self_z,
    )
    x_got = [send(piece, TO_PARTNER) for piece in x_self]
    own_context = context_term(at, after(g, x_self[0]), 0, blocks, F32, 2)
    grad_context = end_context(which, own_context, got_high, got_low)
    outer_grad = (after(zlo_kept, grad_context)[0, :COLS] + zlo_got[0, :COLS].astype(F32)) / 16
    new_momentum = 0.9 * momentum.T + outer_grad
    new_anchor = anchor.T - 0.7 * (outer_grad + 0.9 * new_momentum)
    new_momentum, new_anchor = new_momentum.T, new_anchor.T
    grad_weight, grad_gain = finish(
        at, after(x_got[0], new_anchor, new_momentum), x_got[1], x_self[1], o_self_own, o_mate, o_from_z
    )
    return (grad_context, grad_weight[None], grad_gain, new_anchor, new_momentum)


def solution(mesh):
    placed = (
        P(("replica", "fsdp"), None),
        P(("replica", "fsdp"), None),
        P("replica", "fsdp", None),
        P("replica", None),
        P("replica", "fsdp", None),
        P("fsdp", "replica"),
        P("fsdp", "replica"),
    )
    return jax.shard_map(
        per_device,
        mesh=mesh,
        in_specs=placed,
        out_specs=(
            P(("replica", "fsdp"), None),
            P("replica", "fsdp", None),
            P("replica", None),
            P("fsdp", "replica"),
            P("fsdp", "replica"),
        ),
        check_vma=False,
    )
```

```python
import jax
import jax.numpy as jnp
from jax import lax
from jax.experimental import pallas as pl
from jax.experimental.pallas import tpu as pltpu
from jax.sharding import PartitionSpec as P

BF16 = jnp.bfloat16
F32 = jnp.float32
BOTH = ("replica", "fsdp")
HALF = 1792
COLS = 224
WIDE = 256
TILE = 256
TILES = HALF // TILE
LIMIT = 10 * 2**20


def partner_y(y, core):
    if core == 0:
        return y ^ 1
    return (y - 1) % 4 if y % 2 == 0 else (y + 1) % 4


def table(move):
    pairs = []
    for r in range(16):
        for f in range(8):
            z_lo, x, core, y, z_hi = r // 8, (r // 2) % 4, r % 2, f // 2, f % 2
            z_lo, x, core, y, z_hi = move(z_lo, x, core, y, z_hi)
            pairs.append((r * 8 + f, ((z_lo * 4 + x) * 2 + core) * 8 + y * 2 + z_hi))
    return pairs


TO_PARTNER = table(lambda a, x, c, y, z: (a, x, c, partner_y(y, c), z))
TO_MATE = table(lambda a, x, c, y, z: (a, x, c, partner_y(y, 1 - c), z))
TO_Z = table(lambda a, x, c, y, z: (a, x, c, y, 1 - z))
TO_CORE = table(lambda a, x, c, y, z: (a, x, 1 - c, y, z))
TO_X1 = table(lambda a, x, c, y, z: (a, x ^ 1, c, y, z))
TO_X3 = table(lambda a, x, c, y, z: (a, 3 - x, c, y, z))
TO_ZLO = table(lambda a, x, c, y, z: (1 - a, x, c, y, z))


def send(value, pairs):
    return lax.ppermute(value, BOTH, pairs)


def after(value, *others):
    return lax.optimization_barrier((value, *others))[0]


HELD = pl.BlockSpec(memory_space=pltpu.VMEM)


def near(x):
    return pltpu.with_memory_space_constraint(x, pltpu.VMEM)


def far(x):
    return pltpu.with_memory_space_constraint(x, pltpu.HBM)


def call(kernel, name, cost, out_shape, grid, in_specs, out_specs, scratch=(), aliases=None):
    built = pl.pallas_call(
        kernel,
        out_shape=out_shape,
        grid_spec=pltpu.PrefetchScalarGridSpec(
            num_scalar_prefetch=1,
            grid=grid,
            in_specs=in_specs,
            out_specs=out_specs,
            scratch_shapes=list(scratch),
        ),
        compiler_params=pltpu.CompilerParams(vmem_limit_bytes=LIMIT),
        cost_estimate=pl.CostEstimate(flops=0, bytes_accessed=int(cost * 3e6), transcendentals=0),
        input_output_aliases=aliases or {},
        name=name,
    )

    def run(at, *operands):
        placed = [near(x) if spec is HELD else far(x) for x, spec in zip(operands, in_specs)]
        return built(at, *placed)

    return run


def split_kernel(at_ref, in_ref, own_ref, other_ref, sems):
    copies = []
    rows = own_ref.shape[0] // 4
    for i in range(4):
        for s, (out_ref, half) in enumerate(((own_ref, at_ref[0]), (other_ref, 1 - at_ref[0]))):
            part = pl.ds(i * rows, rows)
            lanes = pl.ds(pl.multiple_of(half * HALF, 256), HALF)
            copies.append(
                pltpu.make_async_copy(in_ref.at[part, lanes], out_ref.at[part], sems.at[s, i])
            )
    for copy in copies:
        copy.start()
    for copy in copies:
        copy.wait()


def split(which, array):
    return call(
        split_kernel,
        "split", 2,
        [pltpu.VMEM((array.shape[0], HALF), BF16)] * 2,
        (1,),
        [pl.BlockSpec(memory_space=pl.ANY)],
        [HELD] * 2,
        [pltpu.SemaphoreType.DMA((2, 4))],
    )(which, array)


def turn_kernel(at_ref, own_ref, high_ref, low_ref, out_ref, slab_ref):
    pieces = ((own_ref, 0, 512), (high_ref, 512, 768), (low_ref, 768, 1024))
    for ref, start, stop in pieces:
        for k in range(8):
            at = pl.ds(pl.multiple_of(at_ref[k] * 256, 256), 256)
            out_ref[k * 256 : (k + 1) * 256, start:stop] = jnp.transpose(ref[:, at])
        at = pl.ds(pl.multiple_of(at_ref[0] * 256, 256), 256)
        slab_ref[start:stop] = ref[:, at]


def turn(at, context, context_p):
    return call(
        turn_kernel,
        "turn", 4,
        [pltpu.VMEM((2048, 1024), BF16), pltpu.VMEM((1024, 256), BF16)],
        (1,),
        [HELD, HELD, HELD],
        [HELD, HELD],
    )(at, context, *context_p)


def outer_parts_kernel(at_ref, delta_ref, low_ref, high_ref, kept_ref):
    rows = pl.ds(pl.multiple_of(pl.program_id(0) * 64, 64), 64)
    for core in range(2):

        @pl.when(at_ref[0] == core)
        def _(core=core):
            for k in range(8):
                away, kept = (2 * k + 1 - core) * COLS, (2 * k + core) * COLS
                away_ref = low_ref if k < 4 else high_ref
                away_ref[k % 4, rows, :COLS] = delta_ref[:, away : away + COLS].astype(BF16)
                kept_ref[k, rows, :COLS] = delta_ref[:, kept : kept + COLS]


def outer_parts(at, delta):
    return call(
        outer_parts_kernel,
        "outer_parts", 3,
        [pltpu.VMEM((4, 256, WIDE), BF16)] * 2 + [pltpu.VMEM((8, 256, WIDE), F32)],
        (4,),
        [pl.BlockSpec((64, 16 * COLS), lambda i, at: (i, 0))],
        [HELD, HELD, HELD],
    )(at, delta)


def outer_sum_kernel(at_ref, kept_in_ref, *refs, turned):
    *got_refs, away_ref, kept_ref = refs
    n = away_ref.shape[0]
    view = jnp.transpose if turned else lambda block: block

    def total(i, at):
        piece = i * len(got_refs) // n
        got = got_refs[piece][at - piece * got_refs[0].shape[0]]
        return view(kept_in_ref[at] + got.astype(F32))

    for i in range(n):
        away_ref[i] = total(i, at_ref[i]).astype(BF16)
        kept_ref[i] = total(i, at_ref[n + i])


def outer_sum(at, kept, *got, turned=False):
    n = at.shape[0] // 2

    def kernel(*refs):
        outer_sum_kernel(*refs, turned=turned)

    return call(
        kernel,
        "outer_sum", 4,
        [pltpu.VMEM((n, 256, WIDE), BF16), pltpu.VMEM((n, 256, WIDE), F32)],
        (1,),
        [HELD] * (1 + len(got)),
        [HELD, HELD],
    )(at, kept, *got)


def slabs(at_ref, block_refs):
    k = 0
    for ref in block_refs:
        for row in range(0, ref.shape[0], 256):
            yield ref, row, pl.ds(pl.multiple_of(at_ref[k] * 256, 256), 256)
            k += 1


def project_kernel(at_ref, own_ref, high_ref, low_ref, *refs):
    *block_refs, out_ref = refs
    pieces = ((own_ref, 0, 512), (high_ref, 512, 768), (low_ref, 768, 1024))
    for j in range(TILES):
        lanes = slice(j * TILE, (j + 1) * TILE)
        for rows_ref, start, stop in pieces:
            total = None
            for ref, row, at in slabs(at_ref, block_refs):
                term = jnp.dot(
                    rows_ref[:, at], ref[row : row + 256, lanes], preferred_element_type=F32
                )
                total = term if total is None else total + term
            out_ref[start:stop, lanes] = total


def project(at, context, context_p, blocks):
    return call(
        project_kernel,
        "project", 14,
        pltpu.VMEM((1024, HALF), F32),
        (1,),
        [HELD] * (3 + len(blocks)),
        HELD,
    )(at, context, *context_p, *blocks)


def gain_lanes(at_ref, j):
    return pl.ds(pl.multiple_of(at_ref[8] * HALF + j * TILE, TILE), TILE)


def stats_kernel(
    at_ref, acc_ref, slab_ref, block_ref, cot_ref, high_ref, low_ref, gain_ref, out_ref
):
    for s in range(4):
        rows = slice(s * 256, (s + 1) * 256)
        part = rows if s < 2 else slice(None)
        c_ref = (cot_ref, cot_ref, high_ref, low_ref)[s]
        squares = jnp.zeros((256, 128), F32)
        products = jnp.zeros((256, 128), F32)
        for j in range(TILES):
            lanes = slice(j * TILE, (j + 1) * TILE)
            p = acc_ref[rows, lanes] + jnp.dot(
                slab_ref[rows], block_ref[:, lanes], preferred_element_type=F32
            )
            scaled = c_ref[part, lanes].astype(F32) * gain_ref[:, gain_lanes(at_ref, j)] * p
            p = p * p
            squares += p[:, :128] + p[:, 128:]
            products += scaled[:, :128] + scaled[:, 128:]
        for i in range(2):
            chunk = slice(i * 128, (i + 1) * 128)
            top = jnp.sum(jnp.transpose(squares[chunk]), axis=0, keepdims=True)
            low = jnp.sum(jnp.transpose(products[chunk]), axis=0, keepdims=True)
            out_ref[2 * s + i] = jnp.concatenate([top] * 4 + [low] * 4, axis=0)


def row_stats(at, acc, slab, block, cot, cot_p, gain):
    return call(
        stats_kernel,
        "row_stats", 3,
        pltpu.VMEM((8, 8, 128), F32),
        (1,),
        [HELD] * 7,
        HELD,
    )(at, acc, slab, block, cot, *cot_p, gain)


def two_parts(value):
    high = value.astype(BF16).astype(F32)
    row = lax.broadcasted_iota(jnp.int32, (16, value.shape[1]), 0)
    return jnp.where(row == 0, high, jnp.where(row == 1, value - high, 0.0)).astype(BF16)


def one_value(rows):
    return jnp.sum(rows.astype(F32), axis=0, keepdims=True)


def grad_kernel(
    at_ref, acc_ref, slab_ref, block_ref, cot_ref, high_ref, low_ref, gain_ref, mine_ref,
    theirs_ref, turned_ref,
    g_ref, x_mate_ref, o_z_ref, a_ref, b_ref,
):
    for i in range(8):
        total = mine_ref[i] + theirs_ref[(i + 4) % 8]
        inverse = lax.rsqrt(total[0:1] / 3584 + 1e-06)
        coupling = total[4:5] / 3584 * inverse * inverse * inverse
        rows = pl.ds(i * 128, 128)
        a_ref[rows, :] = jnp.transpose(jnp.broadcast_to(inverse, (128, 128)))
        b_ref[rows, :] = jnp.transpose(jnp.broadcast_to(coupling, (128, 128)))

    for j in range(TILES):
        lanes = slice(j * TILE, (j + 1) * TILE)
        block = block_ref[:, lanes]
        gain = gain_ref[:, gain_lanes(at_ref, j)]
        gain_total = jnp.zeros((8, TILE), F32)
        for i in range(4):
            rows = slice(i * 256, (i + 1) * 256)
            part = rows if i < 2 else slice(None)
            c_ref = (cot_ref, cot_ref, high_ref, low_ref)[i]
            p = acc_ref[rows, lanes] + jnp.dot(slab_ref[rows], block, preferred_element_type=F32)
            inverse = jnp.concatenate([a_ref[rows]] * 2, axis=1)
            coupling = jnp.concatenate([b_ref[rows]] * 2, axis=1)
            cot = c_ref[part, lanes].astype(F32) * inverse
            g_ref[rows, lanes] = (cot * gain - p * coupling).astype(BF16)
            gain_total += jnp.sum((cot * p).reshape(32, 8, TILE), axis=0)
        terms = jnp.dot(turned_ref[:512], g_ref[:, lanes], preferred_element_type=F32)
        terms = terms.astype(BF16)
        x_mate_ref[:256, lanes] = terms[:256]
        x_mate_ref[256:, lanes] = two_parts(jnp.sum(gain_total, axis=0, keepdims=True))
        o_z_ref[:, lanes] = terms[256:]


def grad_step(at, acc, slab, block, cot, cot_p, gain, mine, theirs, turned):
    return call(
        grad_kernel,
        "grad_step", 6,
        (
            pltpu.VMEM((1024, HALF), BF16),
            pltpu.VMEM((272, HALF), BF16),
            pltpu.VMEM((256, HALF), BF16),
        ),
        (1,),
        [HELD] * 10,
        [HELD] * 3,
        [pltpu.VMEM((1024, 128), F32), pltpu.VMEM((1024, 128), F32)],
    )(at, acc, slab, block, cot, *cot_p, gain, mine, theirs, turned)


def weight_kernel(at_ref, turned_ref, g_ref, *out_refs, first):
    n = len(out_refs)
    for j in range(TILES):
        lanes = slice(j * TILE, (j + 1) * TILE)
        terms = jnp.dot(
            turned_ref[first * 256 : (first + n) * 256],
            g_ref[:, lanes],
            preferred_element_type=F32,
        )
        for k, out_ref in enumerate(out_refs):
            out_ref[:, lanes] = terms[k * 256 : (k + 1) * 256].astype(out_ref.dtype)


def weight_terms(at, turned, g, first, n, dtype):
    def kernel(*refs):
        weight_kernel(*refs, first=first)

    return call(
        kernel,
        "weight_terms", n,
        [pltpu.VMEM((256, HALF), dtype)] * n,
        (1,),
        [HELD, HELD],
        [HELD] * n,
    )(at, turned, g)


def context_kernel(at_ref, g_ref, *refs, first):
    *block_refs, out_ref = refs
    rows = slice(first, first + out_ref.shape[0])
    for ref, row, at in slabs(at_ref, block_refs):
        part = lax.dot_general(
            g_ref[rows, :],
            ref[row : row + 256],
            (((1,), (1,)), ((), ())),
            preferred_element_type=F32,
        )
        out_ref[:, at] = part.astype(out_ref.dtype)


def context_term(at, g, first, blocks, dtype, tiles):
    def kernel(*refs):
        context_kernel(*refs, first=first)

    return call(
        kernel,
        "context_term", 2.5 * tiles,
        pltpu.VMEM((256 * tiles, 2048), dtype),
        (1,),
        [HELD] * (1 + len(blocks)),
        HELD,
    )(at, g, *blocks)


def add_kernel(at_ref, a_ref, b_ref, out_ref):
    out_ref[...] = (a_ref[...] + b_ref[...].astype(F32)).astype(BF16)


def add(at, a, b):
    return call(
        add_kernel, "add", 1, pltpu.VMEM((256, HALF), BF16), (1,), [HELD, HELD], HELD
    )(at, a, b)


def add_x_kernel(at_ref, a_ref, *refs):
    *in_refs, high_ref, low_ref = refs
    sent_ref, *got_refs = in_refs
    total = a_ref[...]
    if got_refs[0].shape[0] == 128:
        got = jnp.concatenate([got_refs[0][...], got_refs[1][:128]], axis=0)
        sums_ref, more = got_refs[1], got_refs[2:]
    else:
        got = got_refs[0][:256]
        sums_ref, more = got_refs[0], got_refs[1:]
    total = total + got.astype(F32)
    for ref in more:
        total = total + ref[...].astype(F32)
    high_ref[...] = total[:128].astype(BF16)
    low_ref[:128] = total[128:].astype(BF16)
    sums = one_value(sent_ref[sent_ref.shape[0] - 16 :])
    low_ref[128:] = two_parts(sums + one_value(sums_ref[sums_ref.shape[0] - 16 :]))


def add_x(at, own, sent, *got):
    return call(
        add_x_kernel,
        "add_x", 1,
        [pltpu.VMEM((128, HALF), BF16), pltpu.VMEM((144, HALF), BF16)],
        (1,),
        [HELD] * (2 + len(got)),
        [HELD, HELD],
    )(at, own, sent, *got)


def end_context_kernel(at_ref, a_ref, b_ref, c_ref, out_ref):
    step = pl.program_id(0)
    rows = pl.ds(pl.multiple_of(step * 128, 128), 128)
    place = pl.ds(pl.multiple_of((step % 2) * 128, 128), 128)

    @pl.when(step < 2)
    def _():
        out_ref[...] = (a_ref[rows, :] + b_ref[place, :].astype(F32)).astype(BF16)

    @pl.when(step >= 2)
    def _():
        out_ref[...] = (a_ref[rows, :] + c_ref[place, :].astype(F32)).astype(BF16)


def end_context(at, own, *got):
    return call(
        end_context_kernel,
        "end_context", 2,
        jax.ShapeDtypeStruct((512, 2048), BF16),
        (4,),
        [HELD, HELD, HELD],
        pl.BlockSpec((128, 2048), lambda i, at: (i, 0)),
    )(at, own, *got)


def finish_kernel(
    at_ref, high_ref, low_ref, sent_ref, o_ref, o_mate_ref, o_z_ref,
    out_ref, gain_ref, own_stage, other_stage, sems,
):
    own = pl.ds(pl.multiple_of(at_ref[8] * HALF, 256), HALF)
    other = pl.ds(pl.multiple_of((1 - at_ref[8]) * HALF, 256), HALF)
    copies = []
    for i in range(4):
        rows = slice(i * 64, (i + 1) * 64)
        x_ref, part = (high_ref, rows) if i < 2 else (low_ref, slice(i * 64 - 128, i * 64 - 64))
        other_stage[rows] = x_ref[part].astype(F32)
        own_stage[rows] = (
            o_ref[rows] + o_mate_ref[rows].astype(F32) + o_z_ref[rows].astype(F32)
        )
        for s, (stage, lanes) in enumerate(((other_stage, other), (own_stage, own))):
            part = pl.ds(i * 64, 64)
            copies.append(
                pltpu.make_async_copy(stage.at[part], out_ref.at[part, lanes], sems.at[s, i])
            )
            copies[-1].start()
    gain_ref[:, own] = one_value(sent_ref[128:])
    gain_ref[:, other] = one_value(low_ref[128:])
    for copy in copies:
        copy.wait()


def finish(at, high, low, sent, o, o_mate, o_z):
    return call(
        finish_kernel,
        "finish", 2,
        [jax.ShapeDtypeStruct((256, 2 * HALF), F32), jax.ShapeDtypeStruct((1, 2 * HALF), F32)],
        (1,),
        [HELD] * 6,
        [
            pl.BlockSpec(memory_space=pl.ANY),
            pl.BlockSpec((1, 2 * HALF), lambda i, at: (0, 0)),
        ],
        [
            pltpu.VMEM((256, HALF), F32),
            pltpu.VMEM((256, HALF), F32),
            pltpu.SemaphoreType.DMA((2, 4)),
        ],
    )(at, high, low, sent, o, o_mate, o_z)


def per_device(context, cotangent, weight, gain, delta, anchor, momentum):
    r = lax.axis_index("replica")
    z_lo, x, core = r // 8, (r // 2) % 4, r % 2
    f = lax.axis_index("fsdp")
    y, z = f // 2, f % 2
    low, high = y ^ 1, jnp.where(y % 2 == 0, (y + 3) % 4, (y + 1) % 4)
    partner = jnp.where(core == 0, low, high)
    mate = jnp.where(core == 0, high, low)
    opposite = (y + 2) % 4
    half = jnp.where(core == 0, ((y + 1) // 2) % 2, y // 2)

    def numbers(*values):
        return jnp.stack([jnp.asarray(value, jnp.int32) for value in values])

    def place(owner, zz):
        return owner * 2 + zz

    turn_order = numbers(
        place(opposite, 1 - z),
        place(mate, 1 - z),
        place(partner, 1 - z),
        place(mate, z),
        place(opposite, z),
        place(y, 1 - z),
        place(partner, z),
        place(y, z),
    )
    at = numbers(
        place(y, z),
        place(mate, z),
        place(partner, z),
        place(y, 1 - z),
        place(opposite, z),
        place(mate, 1 - z),
        place(partner, 1 - z),
        place(opposite, 1 - z),
        half,
    )
    which, which_core = numbers(half), numbers(core)
    x_away, x_pair = x ^ 1, 3 - x
    x1_at = numbers(
        x_away, 3 - x_away, 4 + x_away, 7 - x_away,
        x, x_pair, 4 + x, 4 + x_pair,
    )
    x3_at = numbers(1, 3, 0, 2)
    zlo_at = numbers(1 - z_lo, z_lo)

    own, other = split(which, weight[0])
    own_z = send(own, TO_Z)
    from_mate = send(own, TO_MATE)

    cot, cot_away = split(which, after(cotangent, own))
    core_low, core_high, core_kept = outer_parts(which_core, after(delta[0], own))
    core_got = [send(core_low, TO_CORE), send(core_high, TO_CORE)]
    from_partner = send(after(other, cot_away, core_high), TO_PARTNER)
    from_mate = after(from_mate, own_z, *core_got)

    mate_z = send(from_mate, TO_Z)
    from_partner = after(from_partner, from_mate)
    from_opposite = send(from_partner, TO_MATE)
    partner_z = send(from_partner, TO_Z)
    context_p = [
        send(after(context[:256], core_high), TO_PARTNER),
        send(after(context[256:], core_high), TO_PARTNER),
    ]
    x1_away, x1_kept = outer_sum(x1_at, after(core_kept, from_partner, mate_z), *core_got)
    from_opposite = after(from_opposite, mate_z, x1_away, context_p[0])

    x1_got = send(after(x1_away, from_opposite), TO_X1)
    opposite_z = send(from_opposite, TO_Z)
    cot_p = [
        send(after(cot_away[:256], from_opposite), TO_PARTNER),
        send(after(cot_away[256:], from_opposite), TO_PARTNER),
    ]

    turned, slab = turn(turn_order, context, context_p)
    blocks = [own, from_mate, from_partner, own_z, from_opposite, mate_z, partner_z, opposite_z]
    acc = project(at, after(context, turned), context_p, blocks[:-1])
    last = (at, acc, slab, opposite_z, cot, cot_p, gain)
    mine = row_stats(*last)
    theirs = send(mine, TO_PARTNER)
    x3_away, x3_kept = outer_sum(x3_at, after(x1_kept, mine), x1_got)
    theirs = after(theirs, x3_away)
    g, x_mate_away, o_mate_z = grad_step(*last, mine, theirs, turned)

    x_mate_z = send(x_mate_away, TO_Z)
    o_mate_z = send(o_mate_z, TO_MATE)
    part_p = context_term(at, g, 512, blocks, BF16, 1)
    got_high = send(part_p, TO_PARTNER)
    x_self_z, o_mate = weight_terms(which, turned, after(g, part_p), 2, 2, BF16)
    x_self_z = send(x_self_z, TO_Z)
    x_mate_own, o_self_z_own, x_self_own, o_self_own = weight_terms(
        which, turned, after(g, o_mate), 4, 4, F32
    )


    x_mate = add_x(which, x_mate_own, x_mate_away, after(x_mate_z, x_self_own, o_mate_z))
    x_from_mate = [send(piece, TO_MATE) for piece in x_mate]
    part_p = context_term(at, after(g, x_mate[0]), 768, blocks, BF16, 1)
    got_low = send(part_p, TO_PARTNER)
    o_self_z = add(which, after(o_self_z_own, part_p), o_mate_z)
    o_from_z = send(o_self_z, TO_Z)
    x3_got = send(x3_away, TO_X3)
    zlo_away, zlo_kept = outer_sum(zlo_at, after(x3_kept, o_self_z), x3_got, turned=True)
    zlo_got = send(zlo_away, TO_ZLO)
    o_mate = send(after(o_mate, x_mate[0], got_high), TO_MATE)

    x_self = add_x(
        which,
        x_self_own,
        x_mate[1],
        after(x_from_mate[0], zlo_away),
        x_from_mate[1],
        x_self_z,
    )
    x_got = [send(piece, TO_PARTNER) for piece in x_self]
    own_context = context_term(at, after(g, x_self[0]), 0, blocks, F32, 2)
    grad_context = end_context(which, own_context, got_high, got_low)
    outer_grad = (after(zlo_kept, grad_context)[0, :COLS] + zlo_got[0, :COLS].astype(F32)) / 16
    new_momentum = 0.9 * momentum.T + outer_grad
    new_anchor = anchor.T - 0.7 * (outer_grad + 0.9 * new_momentum)
    new_momentum, new_anchor = new_momentum.T, new_anchor.T
    grad_weight, grad_gain = finish(
        at, after(x_got[0], new_anchor, new_momentum), x_got[1], x_self[1], o_self_own, o_mate, o_from_z
    )
    return (grad_context, grad_weight[None], grad_gain, new_anchor, new_momentum)


def solution(mesh):
    placed = (
        P(("replica", "fsdp"), None),
        P(("replica", "fsdp"), None),
        P("replica", "fsdp", None),
        P("replica", None),
        P("replica", "fsdp", None),
        P("fsdp", "replica"),
        P("fsdp", "replica"),
    )
    return jax.shard_map(
        per_device,
        mesh=mesh,
        in_specs=placed,
        out_specs=(
            P(("replica", "fsdp"), None),
            P("replica", "fsdp", None),
            P("replica", None),
            P("fsdp", "replica"),
            P("fsdp", "replica"),
        ),
        check_vma=False,
    )
```
